32 devices in a mesh: videos: 2 (over y), ha: 4 (over z), wa: 2 (over x), ta: 2 (over core).
Axes of the slice: x: 2, y: 2, z: 4, core: 2. Of those that a mesh axis runs over, the one named last changes fastest.
Arguments:
- latents: bfloat16 [12, 8, 64, 512], P(('videos', 'ta'), 'ha', 'wa'), parts along dimension 0, may hold values from -200 to 200
- norm1_gain: float32 [512], replicated, may hold values from 0.25 to 1.75
- norm1_shift: float32 [512], replicated, may hold values from -2.5 to 2.5
- up_weight: bfloat16 [3, 3, 512, 256], replicated, may hold values from -0.1875 to 0.1875
- norm2_gain: float32 [256], replicated, may hold values from 0.25 to 1.75
- norm2_shift: float32 [256], replicated, may hold values from -2.5 to 2.5
- conv_a: bfloat16 [3, 3, 3, 256, 256], replicated, may hold values from -0.078125 to 0.078125
- norm3_gain: float32 [256], replicated, may hold values from 0.25 to 1.75
- norm3_shift: float32 [256], replicated, may hold values from -2.5 to 2.5
- conv_b: bfloat16 [3, 3, 3, 256, 256], replicated, may hold values from -0.078125 to 0.078125
Outputs:
- decoded: bfloat16 [12, 16, 128, 256], P(('videos', 'ta'), 'ha', 'wa'), parts along dimension 0
The draws below stay inside these ranges and needn't reach their ends.
There are 2 independent parts, one for each index of `videos`. The reference program is written for one: setup_inputs(seed, part) draws one part's arguments, and reference() takes and returns one part's arrays. A program takes and returns all parts, laid end to end along the dimension named above; an argument that names none is the same for every part. Nothing has to cross between parts.
All inputs are finite; a program needn't handle non-finite values.
Results may differ from the reference program's by a relative error of at most 0.008.
Values may be sent and summed in bfloat16 or wider, within the bound.
A program may use at most 64 MiB of HBM per device.

```python
import math
import jax
import jax.numpy as jnp
from jax import lax

C1 = 512
C2 = 256
GROUPS = 32
FRAMES = 6
ROWS = 8
COLS = 64


def draw_latents(key, part):
    keys = jax.random.split(key, 4)
    offsets = jax.random.uniform(keys[0], (C1,), jnp.float32, -1.5, 1.5)
    chan_scale = jnp.exp(jax.random.uniform(keys[1], (C1,), jnp.float32, 0.0, math.log(3.0)))
    pos_scale = jnp.exp(jax.random.uniform(keys[2], (FRAMES, ROWS, COLS, 1), jnp.float32, 0.0, math.log(2.0)))
    ramp = jnp.arange(ROWS, dtype=jnp.float32) / max(ROWS - 1, 1)
    col_ramp = jnp.arange(COLS, dtype=jnp.float32) / max(COLS - 1, 1)
    col_scale = jnp.exp(math.log(2.0) * col_ramp)
    frame_ids = jnp.arange(FRAMES, dtype=jnp.int32)
    early = frame_ids < FRAMES // 2
    frame_gain = jnp.where(early, 0.4, 1.0).astype(jnp.float32)
    frame_shift = jnp.where(early, -0.5, 0.0).astype(jnp.float32)
    noise = jnp.clip(jax.random.normal(keys[3], (FRAMES, ROWS, COLS, C1), jnp.float32), -4.0, 4.0)
    row_scale = 1.0 + 2.0 * ramp
    amplitude = row_scale[None, :, None, None] * col_scale[None, None, :, None] * frame_gain[:, None, None, None]
    values = offsets + frame_shift[:, None, None, None] + noise * amplitude * pos_scale * chan_scale
    return values.astype(jnp.bfloat16)


def normal_values(own_key, extent, scale, limit, kind=jnp.bfloat16):
    entries = jax.random.normal(own_key, extent, jnp.float32) * scale
    return jnp.minimum(jnp.maximum(entries, -limit), limit).astype(kind)


def setup_inputs(seed: int = 0, part: int = 0) -> dict:
    streams_of = jax.random.split(jax.random.key(seed), 11)
    part_splits = jax.random.split(jax.random.fold_in(streams_of[10], part), 11)
    latents = draw_latents(jax.random.fold_in(jax.random.fold_in(streams_of[10], part), 71), part)
    norm1_gain = jnp.clip(1.0 + 0.15 * jax.random.normal(streams_of[1], (C1,), jnp.float32), 0.25, 1.75)
    norm1_shift = normal_values(streams_of[2], (C1,), 0.5, 2.5, jnp.float32)
    up_weight = normal_values(streams_of[3], (3, 3, C1, C2), (2 * C1) ** -0.5, 0.1875)
    norm2_gain = jnp.clip(1.0 + 0.15 * jax.random.normal(streams_of[4], (C2,), jnp.float32), 0.25, 1.75)
    norm2_shift = normal_values(streams_of[5], (C2,), 0.5, 2.5, jnp.float32)
    conv_a = normal_values(streams_of[6], (3, 3, 3, C2, C2), (27 * C2) ** -0.5, 0.078125)
    norm3_gain = jnp.clip(1.0 + 0.15 * jax.random.normal(streams_of[7], (C2,), jnp.float32), 0.25, 1.75)
    norm3_shift = normal_values(streams_of[8], (C2,), 0.5, 2.5, jnp.float32)
    conv_b = normal_values(streams_of[9], (3, 3, 3, C2, C2), (27 * C2) ** -0.5, 0.078125)
    return dict(latents=latents, norm1_gain=norm1_gain, norm1_shift=norm1_shift, up_weight=up_weight, norm2_gain=norm2_gain, norm2_shift=norm2_shift, conv_a=conv_a, norm3_gain=norm3_gain, norm3_shift=norm3_shift, conv_b=conv_b)


EPSILON = 1e-06

def activate(values, scale_vec, shift_vec):
    channels = values.shape[-1]
    group_width = channels // GROUPS
    grouped = values.reshape(-1, GROUPS, group_width)
    average = lax.optimization_barrier(jnp.mean(grouped, axis=(0, 2)))
    centred = grouped - average[None, :, None]
    spread = lax.optimization_barrier(jnp.mean(centred * centred, axis=(0, 2)))
    scaling = 1.0 / jnp.sqrt(spread + EPSILON)
    normed = (values - jnp.repeat(average, group_width)) * jnp.repeat(scaling, group_width) * scale_vec + shift_vec
    return jax.nn.silu(normed).astype(jnp.bfloat16)

def parity_merge(lead_part, mid_part, tail_part, axis_pos):
    pad_end = [(0, 0)] * lead_part.ndim
    pad_front = [(0, 0)] * lead_part.ndim
    pad_end[axis_pos] = (0, 1)
    pad_front[axis_pos] = (1, 0)
    even_part = jnp.pad(lead_part, pad_end) + jnp.pad(tail_part, pad_front)
    odd_part = jnp.pad(mid_part, pad_end)
    stacked = jnp.stack([even_part, odd_part], axis=axis_pos + 1)
    new_shape = list(even_part.shape)
    new_shape[axis_pos] = new_shape[axis_pos] * 2
    return stacked.reshape(new_shape)

def spread_taps(source, kernel):
    frames, height, across, channels = source.shape
    flattened = source.reshape(-1, channels)
    products = [[jnp.dot(flattened, kernel[tap_y, tap_x], preferred_element_type=jnp.float32).reshape(frames, height, across, -1) for tap_x in range(3)] for tap_y in range(3)]
    columns = [parity_merge(products[0][tap_x], products[1][tap_x], products[2][tap_x], 1) for tap_x in range(3)]
    return parity_merge(columns[0], columns[1], columns[2], 2)

def valid_conv(padded, kernel, frames, height, across):
    result = jnp.zeros((frames * height * across, kernel.shape[-1]), jnp.float32)
    for step_t in range(3):
        for step_y in range(3):
            for step_x in range(3):
                window = padded[step_t:step_t + frames, step_y:step_y + height, step_x:step_x + across]
                result = result + jnp.dot(window.reshape(-1, window.shape[-1]), kernel[step_t, step_y, step_x], preferred_element_type=jnp.float32)
    return result.reshape(frames, height, across, -1)

def causal_pad(values):
    extended = jnp.concatenate([values[:1], values[:1], values], axis=0)
    return jnp.pad(extended, ((0, 0), (1, 1), (1, 1), (0, 0)))

def reference(latents, norm1_gain, norm1_shift, up_weight, norm2_gain, norm2_shift, conv_a, norm3_gain, norm3_shift, conv_b):
    frames, height, across, channels = latents.shape
    activated = activate(latents.astype(jnp.float32), norm1_gain, norm1_shift)
    lifted = spread_taps(activated, up_weight)[:, 1:2 * height + 1, 1:2 * across + 1].astype(jnp.bfloat16)
    lifted_f = lifted.astype(jnp.float32)
    first_act = activate(lifted_f, norm2_gain, norm2_shift)
    hidden = valid_conv(causal_pad(first_act), conv_a, frames, 2 * height, 2 * across).astype(jnp.bfloat16)
    second_act = activate(hidden.astype(jnp.float32), norm3_gain, norm3_shift)
    branch = valid_conv(causal_pad(second_act), conv_b, frames, 2 * height, 2 * across)
    return (lifted_f + branch).astype(jnp.bfloat16)
```

```python
import functools
import jax
import jax.numpy as jnp
from jax import lax
from jax.experimental import pallas as pl
from jax.experimental.pallas import tpu as pltpu
from jax.sharding import PartitionSpec as P

GROUPS = 32
EPSILON = 1e-06
MESH = pl.DeviceIdType.MESH
F32 = jnp.float32
BF16 = jnp.bfloat16


def group_sum(x, width):
    pieces = []
    for k in range(x.shape[1] // 128):
        piece = x[:, k * 128 : (k + 1) * 128]
        lane = lax.broadcasted_iota(jnp.int32, piece.shape, 1)
        step = 1
        while step < width:
            ahead = pltpu.roll(piece, 128 - step, 1)
            behind = pltpu.roll(piece, step, 1)
            piece = piece + jnp.where((lane & step) == 0, ahead, behind)
            step *= 2
        pieces.append(piece)
    return jnp.concatenate(pieces, axis=1)


def half_silu(h):
    return h + h * jnp.tanh(h)


def kernel(
    sizes,
    lat,
    g1,
    s1,
    up_hbm,
    g2,
    s2,
    ca_hbm,
    g3,
    s3,
    cb_hbm,
    out,
    up_w,
    ca_w,
    cb_w,
    lat_row,
    lat_col,
    lat_stage,
    up_in,
    raw2,
    raw3,
    col2,
    col3,
    stage2,
    stage3,
    conv_in,
    merged,
    st1,
    st2,
    st3,
    w_sem,
    halo_send,
    halo_recv,
    stat_send,
    stat_recv,
):
    n_ha, n_wa, n_ta = sizes
    n_all = n_ha * n_wa * n_ta
    ha, wa, ta = lax.axis_index("ha"), lax.axis_index("wa"), lax.axis_index("ta")
    me = (ha * n_wa + wa) * n_ta + ta
    frames, height, across, c1 = lat.shape
    c2 = up_w.shape[-1]
    out_h, out_w = 2 * height, 2 * across

    weights = [
        pltpu.make_async_copy(a, b, w_sem.at[i])
        for i, (a, b) in enumerate(((up_hbm, up_w), (ca_hbm, ca_w), (cb_hbm, cb_w)))
    ]
    for w in weights:
        w.start()

    lat_row[...] = jnp.zeros_like(lat_row)
    lat_col[...] = jnp.zeros_like(lat_col)
    for raw, col in ((raw2, col2), (raw3, col3)):
        col[...] = jnp.zeros_like(col)
        for f in range(frames + 2):
            for r in (0, out_h + 1):
                raw[f, r] = jnp.zeros(raw.shape[2:], raw.dtype)

    def peer(d):
        p = lax.rem(me + d, n_all)
        return {"ha": p // (n_wa * n_ta), "wa": (p // n_ta) % n_wa, "ta": p % n_ta}

    barrier = pltpu.get_barrier_semaphore()

    @pl.loop(1, n_all)
    def _(d):
        pl.semaphore_signal(barrier, inc=1, device_id=peer(d), device_id_type=MESH)

    def set_stats(st, x):
        rows = x.shape[0]
        mean = jnp.sum(x, axis=0, keepdims=True) * (1.0 / rows)
        centred = x - mean
        st[0, 0:1, :] = mean
        st[0, 1:2, :] = jnp.sum(centred * centred, axis=0, keepdims=True)

    def send_stats(st, i):
        @pl.loop(1, n_all)
        def _(d):
            pltpu.make_async_remote_copy(
                src_ref=st.at[0],
                dst_ref=st.at[d],
                send_sem=stat_send.at[i],
                recv_sem=stat_recv.at[i],
                device_id=peer(d),
                device_id_type=MESH,
            ).start()

    def all_stats(st, i, sem):
        pltpu.make_async_copy(st.at[1:n_all], st.at[1:n_all], sem.at[i]).wait()

    def affine(st, i, rows, gain, shift):
        all_stats(st, i, stat_recv)
        c = st.shape[-1]
        width = c // GROUPS
        v = st[...]
        mean_c = jnp.broadcast_to(jnp.sum(v, axis=0)[0:1] * (1.0 / n_all), (8, c))
        mean = group_sum(mean_c, width) * (1.0 / width)
        kind = lax.broadcasted_iota(jnp.int32, v.shape, 1)
        off = v - mean[0:2][None]
        parts = jnp.sum(jnp.where(kind == 0, off * off * float(rows), v), axis=0)
        both = jnp.broadcast_to(parts[0:1] + parts[1:2], (8, c))
        spread = group_sum(both, width) * (1.0 / (width * rows * n_all))
        scaling = lax.rsqrt(spread + EPSILON)
        factor = 0.5 * scaling[0:1] * gain[...]
        return mean[0:1], factor, 0.5 * shift[...]

    def inside(dta, dha, dwa):
        h, w, t = ha + dha, wa + dwa, ta + dta
        ok = (h >= 0) & (h < n_ha) & (w >= 0) & (w < n_wa)
        return ok & (t >= 0) & (t < n_ta)

    def neighbour(dta, dha, dwa):
        return {"ha": ha + dha, "wa": wa + dwa, "ta": ta + dta}

    def remote(src, dst, i, move):
        dta, dha, dwa = move
        k = dta * 9 + (dha + 1) * 3 + dwa + 1
        return pltpu.make_async_remote_copy(
            src_ref=src,
            dst_ref=dst,
            send_sem=halo_send.at[i, k],
            recv_sem=halo_recv.at[i, k],
            device_id=neighbour(*move),
            device_id_type=MESH,
        )

    def start(copies):
        for move, copy in copies:
            pl.when(inside(*move))(copy.start)

    def sent(copies):
        for move, copy in copies:
            pl.when(inside(*move))(copy.wait_send)

    def received(copies):
        for move, copy in copies:
            dta, dha, dwa = move
            pl.when(inside(-dta, -dha, -dwa))(copy.wait_recv)

    def field_copies(i, raw, col, stage, dta):
        copies = []
        f_from, f_to, count = (0, 2, frames) if dta == 0 else (frames - 2, 0, 2)
        for dha in (-1, 0, 1):
            r_from, r_to, n_r = {-1: (0, out_h + 1, 1), 0: (0, 1, out_h), 1: (out_h - 1, 0, 1)}[dha]
            for dwa in (0, -1, 1):
                move = (dta, dha, dwa)
                if move == (0, 0, 0):
                    continue
                fd, rd = pl.ds(f_to, count), pl.ds(r_to, n_r)
                if dwa == 0:
                    src = raw.at[pl.ds(f_from + 2, count), pl.ds(r_from + 1, n_r)]
                    dst = raw.at[fd, rd]
                else:
                    side = (dwa + 1) // 2
                    src = stage.at[side, pl.ds(f_from, count), pl.ds(r_from, n_r)]
                    dst = col.at[1 - side, fd, rd]
                copies.append((move, remote(src, dst, i, move)))
        return copies

    set_stats(st1, lat[...].astype(F32).reshape(-1, c1))
    for f in range(frames):
        for r in range(height):
            lat_stage[f, r] = lat[f, r, 0:16, :].astype(F32)[0:1]
    pl.semaphore_wait(barrier, n_all - 1)
    send_stats(st1, 0)
    lat_copies = [
        ((0, -1, 0), remote(lat.at[:, 0], lat_row, 0, (0, -1, 0))),
        ((0, 0, -1), remote(lat_stage, lat_col.at[:, pl.ds(0, height)], 0, (0, 0, -1))),
        (
            (0, -1, -1),
            remote(
                lat_stage.at[:, pl.ds(0, 1)], lat_col.at[:, pl.ds(height, 1)], 0, (0, -1, -1)
            ),
        ),
    ]
    start(lat_copies)
    mean, factor, offset = affine(st1, 0, frames * height * across, g1, s1)
    received(lat_copies)
    row_in = lax.broadcasted_iota(jnp.int32, (across, 1), 0)
    right_ok = (wa < n_wa - 1).astype(F32)
    left_ok = (wa > 0).astype(F32)
    below_ok = (ha < n_ha - 1).astype(F32)
    above_ok = (ha > 0).astype(F32)

    def up_row(f, r, x, keep):
        y = half_silu((x - mean) * factor + offset) * keep
        edge = half_silu((lat_col[f, r] - mean) * factor + offset) * (keep * right_ok)
        moved = jnp.where(row_in == across - 1, edge, pltpu.roll(y, across - 1, 0))
        up_in[f, r, :, 0:c1] = y.astype(BF16)
        up_in[f, r, :, c1 : 2 * c1] = moved.astype(BF16)

    @pl.loop(0, frames)
    def _(f):
        for r in range(height):
            up_row(f, r, lat[f, r].astype(F32), 1.0)
        up_row(f, height, lat_row[f].astype(F32), below_ok)

    weights[0].wait()

    def tap(dy, dx, ky, kx):
        a = up_in[:, dy : dy + height, :, dx * c1 : (dx + 1) * c1].reshape(-1, c1)
        return jnp.dot(a, up_w[ky, kx], preferred_element_type=F32)

    lifted = {
        (0, 0): lambda: tap(0, 0, 1, 1),
        (0, 1): lambda: tap(0, 0, 1, 2) + tap(0, 1, 1, 0),
        (1, 0): lambda: tap(0, 0, 2, 1) + tap(1, 0, 0, 1),
        (1, 1): lambda: tap(0, 0, 2, 2) + tap(0, 1, 2, 0) + tap(1, 0, 0, 2) + tap(1, 1, 0, 0),
    }
    for (a, b), make in lifted.items():
        block = make().astype(BF16).reshape(frames, height, across, c2)
        for i in range(height):
            raw2[2 : 2 + frames, 1 + 2 * i + a, b * across : (b + 1) * across, :] = block[:, i]

    def norm_conv(i, raw, col, stage, st, gain, shift, w, w_copy):
        own = raw[2 : 2 + frames, 1 : 1 + out_h].astype(F32)
        set_stats(st, own.reshape(-1, c2))
        send_stats(st, i)
        for f in range(frames):
            for r in range(out_h):
                stage[0, f, r] = raw[2 + f, 1 + r, 0:16, :].astype(F32)[0:1]
                stage[1, f, r] = raw[2 + f, 1 + r, out_w - 16 : out_w, :].astype(F32)[15:16]
        here = field_copies(i, raw, col, stage, 0)
        later = field_copies(i, raw, col, stage, 1)
        start(later)
        start(here)
        mean, factor, offset = affine(st, i, frames * out_h * out_w, gain, shift)

        def one_row(f, r, keep):
            x = raw[f, r].astype(F32)
            y = half_silu((x - mean) * factor + offset)
            if keep is not None:
                y = y * keep
            even, odd = y[:across], y[across:]
            conv_in[f, r, :, 0:c2] = pltpu.roll(odd, 1, 0).astype(BF16)
            conv_in[f, r, :, c2 : 2 * c2] = even.astype(BF16)
            conv_in[f, r, :, 2 * c2 : 3 * c2] = odd.astype(BF16)
            conv_in[f, r, :, 3 * c2 : 4 * c2] = pltpu.roll(even, across - 1, 0).astype(BF16)

        def edges(f, r, keep):
            first = lax.broadcasted_iota(jnp.int32, (16, 1), 0)
            y = half_silu((col[0, f, r] - mean) * factor + offset) * (keep * left_ok)
            old = conv_in[f, r, 0:16, 0:c2].astype(F32)
            conv_in[f, r, 0:16, 0:c2] = jnp.where(first == 0, y, old).astype(BF16)
            y = half_silu((col[1, f, r] - mean) * factor + offset) * (keep * right_ok)
            old = conv_in[f, r, across - 16 : across, 3 * c2 : 4 * c2].astype(F32)
            conv_in[f, r, across - 16 : across, 3 * c2 : 4 * c2] = jnp.where(
                first == 15, y, old
            ).astype(BF16)

        def finish(f):
            one_row(f, 0, above_ok)
            one_row(f, out_h + 1, below_ok)
            edges(f, 0, above_ok)
            edges(f, out_h + 1, below_ok)
            for r in range(1, out_h + 1):
                edges(f, r, 1.0)

        @pl.loop(2, 2 + frames)
        def _(f):
            for r in range(1, out_h + 1):
                one_row(f, r, None)

        received(here)

        @pl.loop(2, 2 + frames)
        def _(f):
            finish(f)

        @pl.when(ta == 0)
        def _():
            conv_in[0] = conv_in[2]
            conv_in[1] = conv_in[2]

        received(later)

        @pl.when(ta > 0)
        def _():
            @pl.loop(0, 2)
            def _(f):
                for r in range(1, out_h + 1):
                    one_row(f, r, None)
                finish(f)

        w_copy.wait()
        results = []
        for b in range(2):
            total = None
            for dt in range(3):
                for dy in range(3):
                    window = conv_in[
                        dt : dt + frames, dy : dy + out_h, :, b * c2 : (b + 3) * c2
                    ].reshape(-1, 3 * c2)
                    part = jnp.dot(
                        window, w[dt, dy].reshape(3 * c2, c2), preferred_element_type=F32
                    )
                    total = part if total is None else total + part
            results.append(total.reshape(frames, out_h, across, c2))
        return results, here + later

    hidden, copies2 = norm_conv(1, raw2, col2, stage2, st2, g2, s2, ca_w, weights[1])
    for b in range(2):
        raw3[2 : 2 + frames, 1 : 1 + out_h, b * across : (b + 1) * across, :] = hidden[b].astype(
            BF16
        )
    branch, copies3 = norm_conv(2, raw3, col3, stage3, st3, g3, s3, cb_w, weights[2])
    for b in range(2):
        lift = raw2[2 : 2 + frames, 1 : 1 + out_h, b * across : (b + 1) * across, :]
        total = lift.astype(F32) + branch[b]
        for k in range(c2 // 128):
            merged[k, :, :, pl.ds(b, across, stride=2), :] = total[..., k * 128 : (k + 1) * 128]
    for k in range(c2 // 128):
        out[:, :, :, k * 128 : (k + 1) * 128] = merged[k].astype(BF16)

    sent(lat_copies)
    sent(copies2)
    sent(copies3)
    for i, st in enumerate((st1, st2, st3)):
        all_stats(st, i, stat_send)


def per_device(sizes, lat, g1, s1, up_w, g2, s2, ca, g3, s3, cb):
    frames, height, across, c1 = lat.shape
    c2 = up_w.shape[-1]
    out_h, out_w = 2 * height, 2 * across
    n_all = sizes[0] * sizes[1] * sizes[2]
    vmem = pl.BlockSpec(memory_space=pltpu.VMEM)
    hbm = pl.BlockSpec(memory_space=pl.ANY)
    field = pltpu.VMEM((frames + 2, out_h + 2, out_w, c2), BF16)
    column = pltpu.VMEM((2, frames + 2, out_h + 2, 1, c2), F32)
    staged = pltpu.VMEM((2, frames, out_h, 1, c2), F32)
    macs = frames * out_h * out_w * 54 * c2 * c2 + frames * height * across * 9 * c1 * c2
    return pl.pallas_call(
        functools.partial(kernel, sizes),
        out_shape=jax.ShapeDtypeStruct((frames, out_h, out_w, c2), BF16),
        in_specs=[vmem, vmem, vmem, hbm, vmem, vmem, hbm, vmem, vmem, hbm],
        out_specs=vmem,
        scratch_shapes=[
            pltpu.VMEM(up_w.shape, BF16),
            pltpu.VMEM(ca.shape, BF16),
            pltpu.VMEM(cb.shape, BF16),
            pltpu.VMEM((frames, across, c1), BF16),
            pltpu.VMEM((frames, height + 1, 1, c1), F32),
            pltpu.VMEM((frames, height, 1, c1), F32),
            pltpu.VMEM((frames, height + 1, across, 2 * c1), BF16),
            field,
            field,
            column,
            column,
            staged,
            staged,
            pltpu.VMEM((frames + 2, out_h + 2, across, 4 * c2), BF16),
            pltpu.VMEM((c2 // 128, frames, out_h, out_w, 128), F32),
            pltpu.VMEM((n_all, 2, c1), F32),
            pltpu.VMEM((n_all, 2, c2), F32),
            pltpu.VMEM((n_all, 2, c2), F32),
            pltpu.SemaphoreType.DMA((3,)),
            pltpu.SemaphoreType.DMA((3, 18)),
            pltpu.SemaphoreType.DMA((3, 18)),
            pltpu.SemaphoreType.DMA((3,)),
            pltpu.SemaphoreType.DMA((3,)),
        ],
        compiler_params=pltpu.CompilerParams(
            collective_id=0, has_side_effects=True, vmem_limit_bytes=44 * 2**20
        ),
        cost_estimate=pl.CostEstimate(
            flops=2 * macs, bytes_accessed=10_000_000, transcendentals=2_000_000
        ),
    )(lat, g1[None], s1[None], up_w, g2[None], s2[None], ca, g3[None], s3[None], cb)


def solution(mesh):
    sizes = (mesh.shape["ha"], mesh.shape["wa"], mesh.shape["ta"])
    fields = P(("videos", "ta"), "ha", "wa", None)
    return jax.shard_map(
        functools.partial(per_device, sizes),
        mesh=mesh,
        in_specs=(fields,) + (P(),) * 9,
        out_specs=fields,
        check_vma=False,
    )
```

```python
import functools
import jax
import jax.numpy as jnp
from jax import lax
from jax.experimental import pallas as pl
from jax.experimental.pallas import tpu as pltpu
from jax.sharding import PartitionSpec as P

GROUPS = 32
EPSILON = 1e-06
MESH = pl.DeviceIdType.MESH
F32 = jnp.float32
BF16 = jnp.bfloat16


def group_sum(x, width):
    pieces = []
    for k in range(x.shape[1] // 128):
        piece = x[:, k * 128 : (k + 1) * 128]
        lane = lax.broadcasted_iota(jnp.int32, piece.shape, 1)
        step = 1
        while step < width:
            ahead = pltpu.roll(piece, 128 - step, 1)
            behind = pltpu.roll(piece, step, 1)
            piece = piece + jnp.where((lane & step) == 0, ahead, behind)
            step *= 2
        pieces.append(piece)
    return jnp.concatenate(pieces, axis=1)


def half_silu(h):
    return h + h * jnp.tanh(h)


def kernel(
    sizes,
    lat_hbm,
    g1_hbm,
    s1_hbm,
    up_hbm,
    g2_hbm,
    s2_hbm,
    ca_hbm,
    g3_hbm,
    s3_hbm,
    cb_hbm,
    out,
    lat,
    g1,
    s1,
    up_w,
    g2,
    s2,
    ca_w,
    g3,
    s3,
    cb_w,
    lat_row,
    lat_col,
    lat_stage,
    up_in,
    raw2,
    raw3,
    col2,
    col3,
    stage2,
    stage3,
    conv_in,
    merged,
    st1,
    st2,
    st3,
    w_sem,
    halo_send,
    halo_recv,
    stat_send,
    stat_recv,
):
    n_ha, n_wa, n_ta = sizes
    n_all = n_ha * n_wa * n_ta
    ha, wa, ta = lax.axis_index("ha"), lax.axis_index("wa"), lax.axis_index("ta")
    frames, height, across, c1 = lat.shape
    c2 = up_w.shape[-1]
    out_h, out_w = 2 * height, 2 * across

    sources = (lat_hbm, up_hbm, g1_hbm, s1_hbm, g2_hbm, s2_hbm, g3_hbm, s3_hbm, ca_hbm, cb_hbm)
    places = (lat, up_w, g1, s1, g2, s2, g3, s3, ca_w, cb_w)
    fetches = [
        pltpu.make_async_copy(a, b, w_sem.at[i]) for i, (a, b) in enumerate(zip(sources, places))
    ]
    for fetch in fetches:
        fetch.start()

    lat_row[...] = jnp.zeros_like(lat_row)
    lat_col[...] = jnp.zeros_like(lat_col)
    for raw, col in ((raw2, col2), (raw3, col3)):
        col[...] = jnp.zeros_like(col)
        for f in range(frames + 2):
            for r in (0, out_h + 1):
                raw[f, r] = jnp.zeros(raw.shape[2:], raw.dtype)

    at_ha = [ha if d == 0 else lax.rem(ha + d, n_ha) for d in range(n_ha)]
    at_wa = [wa if d == 0 else lax.rem(wa + d, n_wa) for d in range(n_wa)]
    at_ta = [ta if d == 0 else lax.rem(ta + d, n_ta) for d in range(n_ta)]

    def peers():
        for slot in range(n_all - 1, 0, -1):
            h, w, t = slot // (n_wa * n_ta), slot // n_ta % n_wa, slot % n_ta
            yield slot, {"ha": at_ha[h], "wa": at_wa[w], "ta": at_ta[t]}

    barrier = pltpu.get_barrier_semaphore()
    for _, device in peers():
        pl.semaphore_signal(barrier, inc=1, device_id=device, device_id_type=MESH)

    def set_stats(st, x):
        rows = x.shape[0]
        mean = jnp.sum(x, axis=0, keepdims=True) * (1.0 / rows)
        centred = x - mean
        st[0, 0:1, :] = mean
        st[0, 1:2, :] = jnp.sum(centred * centred, axis=0, keepdims=True)

    def send_stats(st, i):
        for slot, device in peers():
            pltpu.make_async_remote_copy(
                src_ref=st.at[0],
                dst_ref=st.at[slot],
                send_sem=stat_send.at[i],
                recv_sem=stat_recv.at[i],
                device_id=device,
                device_id_type=MESH,
            ).start()

    def all_stats(st, i, sem):
        pltpu.make_async_copy(st.at[1:n_all], st.at[1:n_all], sem.at[i]).wait()

    def affine(st, i, rows, gain, shift):
        all_stats(st, i, stat_recv)
        c = st.shape[-1]
        width = c // GROUPS
        v = st[...]
        mean_c = jnp.broadcast_to(jnp.sum(v, axis=0)[0:1] * (1.0 / n_all), (8, c))
        mean = group_sum(mean_c, width) * (1.0 / width)
        kind = lax.broadcasted_iota(jnp.int32, v.shape, 1)
        off = v - mean[0:2][None]
        parts = jnp.sum(jnp.where(kind == 0, off * off * float(rows), v), axis=0)
        both = jnp.broadcast_to(parts[0:1] + parts[1:2], (8, c))
        spread = group_sum(both, width) * (1.0 / (width * rows * n_all))
        scaling = lax.rsqrt(spread + EPSILON)
        factor = 0.5 * scaling[0:1] * gain[...]
        return mean[0:1], factor, 0.5 * shift[...]

    def inside(dta, dha, dwa):
        h, w, t = ha + dha, wa + dwa, ta + dta
        ok = (h >= 0) & (h < n_ha) & (w >= 0) & (w < n_wa)
        return ok & (t >= 0) & (t < n_ta)

    def neighbour(dta, dha, dwa):
        return {"ha": ha + dha, "wa": wa + dwa, "ta": ta + dta}

    def remote(src, dst, i, move):
        dta, dha, dwa = move
        k = dta * 9 + (dha + 1) * 3 + dwa + 1
        return pltpu.make_async_remote_copy(
            src_ref=src,
            dst_ref=dst,
            send_sem=halo_send.at[i, k],
            recv_sem=halo_recv.at[i, k],
            device_id=neighbour(*move),
            device_id_type=MESH,
        )

    def start(copies):
        for move, copy in copies:
            pl.when(inside(*move))(copy.start)

    def sent(copies):
        for move, copy in copies:
            pl.when(inside(*move))(copy.wait_send)

    def received(copies):
        for move, copy in copies:
            dta, dha, dwa = move
            pl.when(inside(-dta, -dha, -dwa))(copy.wait_recv)

    def field_copies(i, raw, col, stage, dta):
        copies = []
        f_from, f_to, count = (0, 2, frames) if dta == 0 else (frames - 2, 0, 2)
        for dha in (-1, 0, 1):
            r_from, r_to, n_r = {-1: (0, out_h + 1, 1), 0: (0, 1, out_h), 1: (out_h - 1, 0, 1)}[dha]
            for dwa in (0, -1, 1):
                move = (dta, dha, dwa)
                if move == (0, 0, 0):
                    continue
                fd, rd = pl.ds(f_to, count), pl.ds(r_to, n_r)
                if dwa == 0:
                    src = raw.at[pl.ds(f_from + 2, count), pl.ds(r_from + 1, n_r)]
                    dst = raw.at[fd, rd]
                else:
                    side = (dwa + 1) // 2
                    src = stage.at[side, pl.ds(f_from, count), pl.ds(r_from, n_r)]
                    dst = col.at[1 - side, fd, rd]
                copies.append((move, remote(src, dst, i, move)))
        return copies

    fetches[0].wait()
    set_stats(st1, lat[...].astype(F32).reshape(-1, c1))
    for f in range(frames):
        for r in range(height):
            lat_stage[f, r] = lat[f, r, 0:16, :].astype(F32)[0:1]
    pl.semaphore_wait(barrier, n_all - 1)
    send_stats(st1, 0)
    lat_copies = [
        ((0, -1, 0), remote(lat.at[:, 0], lat_row, 0, (0, -1, 0))),
        ((0, 0, -1), remote(lat_stage, lat_col.at[:, pl.ds(0, height)], 0, (0, 0, -1))),
        (
            (0, -1, -1),
            remote(
                lat_stage.at[:, pl.ds(0, 1)], lat_col.at[:, pl.ds(height, 1)], 0, (0, -1, -1)
            ),
        ),
    ]
    start(lat_copies)
    for fetch in fetches[2:8]:
        fetch.wait()
    mean, factor, offset = affine(st1, 0, frames * height * across, g1, s1)
    received(lat_copies)
    row_in = lax.broadcasted_iota(jnp.int32, (across, 1), 0)
    right_ok = (wa < n_wa - 1).astype(F32)
    left_ok = (wa > 0).astype(F32)
    below_ok = (ha < n_ha - 1).astype(F32)
    above_ok = (ha > 0).astype(F32)

    def up_row(f, r, x, keep):
        y = half_silu((x - mean) * factor + offset) * keep
        edge = half_silu((lat_col[f, r] - mean) * factor + offset) * (keep * right_ok)
        moved = jnp.where(row_in == across - 1, edge, pltpu.roll(y, across - 1, 0))
        up_in[f, r, :, 0:c1] = y.astype(BF16)
        up_in[f, r, :, c1 : 2 * c1] = moved.astype(BF16)

    @pl.loop(0, frames)
    def _(f):
        for r in range(height):
            up_row(f, r, lat[f, r].astype(F32), 1.0)
        up_row(f, height, lat_row[f].astype(F32), below_ok)

    fetches[1].wait()

    def tap(dy, dx, ky, kx):
        a = up_in[:, dy : dy + height, :, dx * c1 : (dx + 1) * c1].reshape(-1, c1)
        return jnp.dot(a, up_w[ky, kx], preferred_element_type=F32)

    lifted = {
        (0, 0): lambda: tap(0, 0, 1, 1),
        (0, 1): lambda: tap(0, 0, 1, 2) + tap(0, 1, 1, 0),
        (1, 0): lambda: tap(0, 0, 2, 1) + tap(1, 0, 0, 1),
        (1, 1): lambda: tap(0, 0, 2, 2) + tap(0, 1, 2, 0) + tap(1, 0, 0, 2) + tap(1, 1, 0, 0),
    }
    for (a, b), make in lifted.items():
        block = make().astype(BF16).reshape(frames, height, across, c2)
        for i in range(height):
            raw2[2 : 2 + frames, 1 + 2 * i + a, b * across : (b + 1) * across, :] = block[:, i]

    def norm_conv(i, raw, col, stage, st, gain, shift, w, w_copy):
        own = raw[2 : 2 + frames, 1 : 1 + out_h].astype(F32)
        set_stats(st, own.reshape(-1, c2))
        send_stats(st, i)
        for f in range(frames):
            for r in range(out_h):
                stage[0, f, r] = raw[2 + f, 1 + r, 0:16, :].astype(F32)[0:1]
                stage[1, f, r] = raw[2 + f, 1 + r, out_w - 16 : out_w, :].astype(F32)[15:16]
        here = field_copies(i, raw, col, stage, 0)
        later = field_copies(i, raw, col, stage, 1)
        start(later)
        start(here)
        mean, factor, offset = affine(st, i, frames * out_h * out_w, gain, shift)

        def one_row(f, r, keep):
            x = raw[f, r].astype(F32)
            y = half_silu((x - mean) * factor + offset)
            if keep is not None:
                y = y * keep
            even, odd = y[:across], y[across:]
            conv_in[f, r, :, 0:c2] = pltpu.roll(odd, 1, 0).astype(BF16)
            conv_in[f, r, :, c2 : 2 * c2] = even.astype(BF16)
            conv_in[f, r, :, 2 * c2 : 3 * c2] = odd.astype(BF16)
            conv_in[f, r, :, 3 * c2 : 4 * c2] = pltpu.roll(even, across - 1, 0).astype(BF16)

        def edges(f, r, keep):
            first = lax.broadcasted_iota(jnp.int32, (16, 1), 0)
            y = half_silu((col[0, f, r] - mean) * factor + offset) * (keep * left_ok)
            old = conv_in[f, r, 0:16, 0:c2].astype(F32)
            conv_in[f, r, 0:16, 0:c2] = jnp.where(first == 0, y, old).astype(BF16)
            y = half_silu((col[1, f, r] - mean) * factor + offset) * (keep * right_ok)
            old = conv_in[f, r, across - 16 : across, 3 * c2 : 4 * c2].astype(F32)
            conv_in[f, r, across - 16 : across, 3 * c2 : 4 * c2] = jnp.where(
                first == 15, y, old
            ).astype(BF16)

        def finish(f):
            one_row(f, 0, above_ok)
            one_row(f, out_h + 1, below_ok)
            edges(f, 0, above_ok)
            edges(f, out_h + 1, below_ok)
            for r in range(1, out_h + 1):
                edges(f, r, 1.0)

        @pl.loop(2, 2 + frames)
        def _(f):
            for r in range(1, out_h + 1):
                one_row(f, r, None)

        received(here)

        @pl.loop(2, 2 + frames)
        def _(f):
            finish(f)

        @pl.when(ta == 0)
        def _():
            conv_in[0] = conv_in[2]
            conv_in[1] = conv_in[2]

        received(later)

        @pl.when(ta > 0)
        def _():
            @pl.loop(0, 2)
            def _(f):
                for r in range(1, out_h + 1):
                    one_row(f, r, None)
                finish(f)

        w_copy.wait()
        results = []
        for b in range(2):
            total = None
            for dt in range(3):
                for dy in range(3):
                    window = conv_in[
                        dt : dt + frames, dy : dy + out_h, :, b * c2 : (b + 3) * c2
                    ].reshape(-1, 3 * c2)
                    part = jnp.dot(
                        window, w[dt, dy].reshape(3 * c2, c2), preferred_element_type=F32
                    )
                    total = part if total is None else total + part
            results.append(total.reshape(frames, out_h, across, c2))
        return results, here + later

    hidden, copies2 = norm_conv(1, raw2, col2, stage2, st2, g2, s2, ca_w, fetches[8])
    for b in range(2):
        raw3[2 : 2 + frames, 1 : 1 + out_h, b * across : (b + 1) * across, :] = hidden[b].astype(
            BF16
        )
    branch, copies3 = norm_conv(2, raw3, col3, stage3, st3, g3, s3, cb_w, fetches[9])
    for b in range(2):
        lift = raw2[2 : 2 + frames, 1 : 1 + out_h, b * across : (b + 1) * across, :]
        total = lift.astype(F32) + branch[b]
        for k in range(c2 // 128):
            merged[k, :, :, pl.ds(b, across, stride=2), :] = total[..., k * 128 : (k + 1) * 128]
    for k in range(c2 // 128):
        out[:, :, :, k * 128 : (k + 1) * 128] = merged[k].astype(BF16)

    sent(lat_copies)
    sent(copies2)
    sent(copies3)
    for i, st in enumerate((st1, st2, st3)):
        all_stats(st, i, stat_send)


def per_device(sizes, lat, g1, s1, up_w, g2, s2, ca, g3, s3, cb):
    frames, height, across, c1 = lat.shape
    c2 = up_w.shape[-1]
    out_h, out_w = 2 * height, 2 * across
    n_all = sizes[0] * sizes[1] * sizes[2]
    vmem = pl.BlockSpec(memory_space=pltpu.VMEM)
    hbm = pl.BlockSpec(memory_space=pltpu.HBM)
    field = pltpu.VMEM((frames + 2, out_h + 2, out_w, c2), BF16)
    column = pltpu.VMEM((2, frames + 2, out_h + 2, 1, c2), F32)
    staged = pltpu.VMEM((2, frames, out_h, 1, c2), F32)
    macs = frames * out_h * out_w * 54 * c2 * c2 + frames * height * across * 9 * c1 * c2
    return pl.pallas_call(
        functools.partial(kernel, sizes),
        out_shape=jax.ShapeDtypeStruct((frames, out_h, out_w, c2), BF16),
        in_specs=[hbm] * 10,
        out_specs=vmem,
        scratch_shapes=[
            pltpu.VMEM(lat.shape, BF16),
            pltpu.VMEM((1, c1), F32),
            pltpu.VMEM((1, c1), F32),
            pltpu.VMEM(up_w.shape, BF16),
            pltpu.VMEM((1, c2), F32),
            pltpu.VMEM((1, c2), F32),
            pltpu.VMEM(ca.shape, BF16),
            pltpu.VMEM((1, c2), F32),
            pltpu.VMEM((1, c2), F32),
            pltpu.VMEM(cb.shape, BF16),
            pltpu.VMEM((frames, across, c1), BF16),
            pltpu.VMEM((frames, height + 1, 1, c1), F32),
            pltpu.VMEM((frames, height, 1, c1), F32),
            pltpu.VMEM((frames, height + 1, across, 2 * c1), BF16),
            field,
            field,
            column,
            column,
            staged,
            staged,
            pltpu.VMEM((frames + 2, out_h + 2, across, 4 * c2), BF16),
            pltpu.VMEM((c2 // 128, frames, out_h, out_w, 128), F32),
            pltpu.VMEM((n_all, 2, c1), F32),
            pltpu.VMEM((n_all, 2, c2), F32),
            pltpu.VMEM((n_all, 2, c2), F32),
            pltpu.SemaphoreType.DMA((10,)),
            pltpu.SemaphoreType.DMA((3, 18)),
            pltpu.SemaphoreType.DMA((3, 18)),
            pltpu.SemaphoreType.DMA((3,)),
            pltpu.SemaphoreType.DMA((3,)),
        ],
        compiler_params=pltpu.CompilerParams(
            collective_id=0, has_side_effects=True, vmem_limit_bytes=63 * 2**20
        ),
        cost_estimate=pl.CostEstimate(
            flops=2 * macs, bytes_accessed=10_000_000, transcendentals=2_000_000
        ),
    )(lat, g1[None], s1[None], up_w, g2[None], s2[None], ca, g3[None], s3[None], cb)


def solution(mesh):
    sizes = (mesh.shape["ha"], mesh.shape["wa"], mesh.shape["ta"])
    fields = P(("videos", "ta"), "ha", "wa", None)
    return jax.shard_map(
        functools.partial(per_device, sizes),
        mesh=mesh,
        in_specs=(fields,) + (P(),) * 9,
        out_specs=fields,
        check_vma=False,
    )
```

```python
import functools
import jax
import jax.numpy as jnp
from jax import lax
from jax.experimental import pallas as pl
from jax.experimental.pallas import tpu as pltpu
from jax.sharding import PartitionSpec as P

GROUPS = 32
EPSILON = 1e-06
MESH = pl.DeviceIdType.MESH
F32 = jnp.float32
BF16 = jnp.bfloat16


def group_moments(mean, squares, count, width):
    means, totals = [], []
    for k in range(mean.shape[1] // 128):
        m, q = (v[:, k * 128 : (k + 1) * 128] for v in (mean, squares))
        lane = lax.broadcasted_iota(jnp.int32, m.shape, 1)
        step = 1
        while step < width:
            low = (lane & step) == 0
            m_other, q_other = (
                jnp.where(low, pltpu.roll(v, 128 - step, 1), pltpu.roll(v, step, 1)) for v in (m, q)
            )
            gap = m - m_other
            q = q + q_other + gap * gap * (0.5 * count * step)
            m = 0.5 * (m + m_other)
            step *= 2
        means.append(m)
        totals.append(q)
    return jnp.concatenate(means, axis=1), jnp.concatenate(totals, axis=1)


def half_silu(h):
    return h + h * jnp.tanh(h)


def kernel(
    sizes,
    lat_hbm,
    g1_hbm,
    s1_hbm,
    up_hbm,
    g2_hbm,
    s2_hbm,
    ca_hbm,
    g3_hbm,
    s3_hbm,
    cb_hbm,
    out,
    lat,
    g1,
    s1,
    up_w,
    g2,
    s2,
    ca_w,
    g3,
    s3,
    cb_w,
    lat_row,
    lat_col,
    lat_stage,
    up_in,
    raw2,
    raw3,
    col2,
    col3,
    stage2,
    stage3,
    conv_in,
    acc,
    merged,
    st1,
    st2,
    st3,
    w_sem,
    halo_send,
    halo_recv,
    stat_send,
    stat_recv,
):
    n_ha, n_wa, n_ta = sizes
    n_all = n_ha * n_wa * n_ta
    ha, wa, ta = lax.axis_index("ha"), lax.axis_index("wa"), lax.axis_index("ta")
    frames, height, across, c1 = lat.shape
    c2 = up_w.shape[-1]
    out_h, out_w = 2 * height, 2 * across

    sources = (lat_hbm, up_hbm, g1_hbm, s1_hbm, g2_hbm, s2_hbm, g3_hbm, s3_hbm, ca_hbm, cb_hbm)
    places = (lat, up_w, g1, s1, g2, s2, g3, s3, ca_w, cb_w)
    fetches = [
        pltpu.make_async_copy(a, b, w_sem.at[i]) for i, (a, b) in enumerate(zip(sources, places))
    ]
    fetches[0].start()
    for fetch in fetches[2:8]:
        fetch.start()

    at_ha = [ha if d == 0 else lax.rem(ha + d, n_ha) for d in range(n_ha)]
    at_wa = [wa if d == 0 else lax.rem(wa + d, n_wa) for d in range(n_wa)]
    at_ta = [ta if d == 0 else lax.rem(ta + d, n_ta) for d in range(n_ta)]

    def peers():
        for slot in range(n_all - 1, 0, -1):
            h, w, t = slot // (n_wa * n_ta), slot // n_ta % n_wa, slot % n_ta
            yield slot, {"ha": at_ha[h], "wa": at_wa[w], "ta": at_ta[t]}

    barrier = pltpu.get_barrier_semaphore()
    for _, device in peers():
        pl.semaphore_signal(barrier, inc=1, device_id=device, device_id_type=MESH)

    def set_stats(st, x):
        rows = x.shape[0]
        mean = jnp.sum(x, axis=0, keepdims=True) * (1.0 / rows)
        centred = x - mean
        st[0, 0:1, :] = mean
        st[0, 1:2, :] = jnp.sum(centred * centred, axis=0, keepdims=True)

    def send_stats(st, i):
        for slot, device in peers():
            pltpu.make_async_remote_copy(
                src_ref=st.at[0],
                dst_ref=st.at[slot],
                send_sem=stat_send.at[i],
                recv_sem=stat_recv.at[i],
                device_id=device,
                device_id_type=MESH,
            ).start()

    def all_stats(st, i, sem):
        pltpu.make_async_copy(st.at[1:n_all], st.at[1:n_all], sem.at[i]).wait()

    def affine(st, i, rows, gain, shift):
        all_stats(st, i, stat_recv)
        c = st.shape[-1]
        width = c // GROUPS
        v = st[...]
        mean_c = jnp.sum(v, axis=0) * (1.0 / n_all)
        kind = lax.broadcasted_iota(jnp.int32, v.shape, 1)
        off = v - mean_c[0:1][None]
        parts = jnp.sum(jnp.where(kind == 0, off * off * float(rows), v), axis=0)
        mean, squares = group_moments(
            jnp.broadcast_to(mean_c[0:1], (8, c)),
            jnp.broadcast_to(parts[0:1] + parts[1:2], (8, c)),
            float(rows * n_all),
            width,
        )
        spread = squares * (1.0 / (width * rows * n_all))
        scaling = lax.rsqrt(spread + EPSILON)
        factor = 0.5 * scaling[0:1] * gain[...]
        return mean[0:1], factor, 0.5 * shift[...]

    def inside(dta, dha, dwa):
        h, w, t = ha + dha, wa + dwa, ta + dta
        ok = (h >= 0) & (h < n_ha) & (w >= 0) & (w < n_wa)
        return ok & (t >= 0) & (t < n_ta)

    def neighbour(dta, dha, dwa):
        return {"ha": ha + dha, "wa": wa + dwa, "ta": ta + dta}

    def remote(src, dst, i, move):
        dta, dha, dwa = move
        k = dta * 9 + (dha + 1) * 3 + dwa + 1
        return pltpu.make_async_remote_copy(
            src_ref=src,
            dst_ref=dst,
            send_sem=halo_send.at[i, k],
            recv_sem=halo_recv.at[i, k],
            device_id=neighbour(*move),
            device_id_type=MESH,
        )

    def start(copies):
        for move, copy in copies:
            pl.when(inside(*move))(copy.start)

    def sent(copies):
        for move, copy in copies:
            pl.when(inside(*move))(copy.wait_send)

    def received(copies):
        for move, copy in copies:
            dta, dha, dwa = move
            pl.when(inside(-dta, -dha, -dwa))(copy.wait_recv)

    def field_copies(i, raw, col, stage, dta):
        copies = []
        f_from, f_to, count = (0, 2, frames) if dta == 0 else (frames - 2, 0, 2)
        for dha in (-1, 0, 1):
            r_from, r_to, n_r = {-1: (0, out_h + 1, 1), 0: (0, 1, out_h), 1: (out_h - 1, 0, 1)}[dha]
            for dwa in (0, -1, 1):
                move = (dta, dha, dwa)
                if move == (0, 0, 0):
                    continue
                fd, rd = pl.ds(f_to, count), pl.ds(r_to, n_r)
                if dwa == 0:
                    src = raw.at[pl.ds(f_from + 2, count), pl.ds(r_from + 1, n_r)]
                    dst = raw.at[fd, rd]
                else:
                    side = (dwa + 1) // 2
                    src = stage.at[side, pl.ds(f_from, count), pl.ds(r_from, n_r)]
                    dst = col.at[1 - side, fd, rd]
                copies.append((move, remote(src, dst, i, move)))
        return copies

    fetches[0].wait()
    for i in (1, 8, 9):
        fetches[i].start()
    set_stats(st1, lat[...].astype(F32).reshape(-1, c1))
    for f in range(frames):
        for r in range(height):
            lat_stage[f, r] = lat[f, r, 0:16, :].astype(F32)[0:1]
    pl.semaphore_wait(barrier, n_all - 1)
    send_stats(st1, 0)
    lat_copies = [
        ((0, -1, 0), remote(lat.at[:, 0], lat_row, 0, (0, -1, 0))),
        ((0, 0, -1), remote(lat_stage, lat_col.at[:, pl.ds(0, height)], 0, (0, 0, -1))),
        (
            (0, -1, -1),
            remote(
                lat_stage.at[:, pl.ds(0, 1)], lat_col.at[:, pl.ds(height, 1)], 0, (0, -1, -1)
            ),
        ),
    ]
    start(lat_copies)
    for fetch in fetches[2:8]:
        fetch.wait()
    mean, factor, offset = affine(st1, 0, frames * height * across, g1, s1)
    received(lat_copies)
    row_in = lax.broadcasted_iota(jnp.int32, (across, 1), 0)
    right_ok, left_ok = wa < n_wa - 1, wa > 0
    below_ok, above_ok = ha < n_ha - 1, ha > 0

    def up_row(f, r, x, keep):
        y = half_silu((x - mean) * factor + offset)
        edge = half_silu((lat_col[f, r] - mean) * factor + offset)
        edge = jnp.where(right_ok, edge, 0.0)
        moved = jnp.where(row_in == across - 1, edge, pltpu.roll(y, across - 1, 0))
        if keep is not None:
            y, moved = jnp.where(keep, y, 0.0), jnp.where(keep, moved, 0.0)
        up_in[f, r, :, 0:c1] = y.astype(BF16)
        up_in[f, r, :, c1 : 2 * c1] = moved.astype(BF16)

    @pl.loop(0, frames)
    def _(f):
        for r in range(height):
            up_row(f, r, lat[f, r].astype(F32), None)
        up_row(f, height, lat_row[f].astype(F32), below_ok)

    fetches[1].wait()

    def tap(dy, dx, ky, kx):
        a = up_in[:, dy : dy + height, :, dx * c1 : (dx + 1) * c1].reshape(-1, c1)
        return jnp.dot(a, up_w[ky, kx], preferred_element_type=F32)

    lifted = {
        (0, 0): lambda: tap(0, 0, 1, 1),
        (0, 1): lambda: tap(0, 0, 1, 2) + tap(0, 1, 1, 0),
        (1, 0): lambda: tap(0, 0, 2, 1) + tap(1, 0, 0, 1),
        (1, 1): lambda: tap(0, 0, 2, 2) + tap(0, 1, 2, 0) + tap(1, 0, 0, 2) + tap(1, 1, 0, 0),
    }
    for (a, b), make in lifted.items():
        block = make().astype(BF16).reshape(frames, height, across, c2)
        for i in range(height):
            raw2[2 : 2 + frames, 1 + 2 * i + a, b * across : (b + 1) * across, :] = block[:, i]

    def norm_conv(i, raw, col, stage, st, gain, shift, w, w_copy):
        own = raw[2 : 2 + frames, 1 : 1 + out_h].astype(F32)
        set_stats(st, own.reshape(-1, c2))
        send_stats(st, i)
        copies = field_copies(i, raw, col, stage, 1) + field_copies(i, raw, col, stage, 0)
        start([c for c in copies if c[0][2] == 0 and c[0][1] != 0])
        start([c for c in copies if c[0][2] == 0 and c[0][1] == 0])
        for f in range(frames):
            for r in range(out_h):
                stage[0, f, r] = raw[2 + f, 1 + r, 0:16, :].astype(F32)[0:1]
                stage[1, f, r] = raw[2 + f, 1 + r, out_w - 16 : out_w, :].astype(F32)[15:16]
        start([c for c in copies if c[0][2] != 0 and c[0][1] == 0])
        start([c for c in copies if c[0][2] != 0 and c[0][1] != 0])
        mean, factor, offset = affine(st, i, frames * out_h * out_w, gain, shift)

        def act(x):
            return half_silu((x - mean) * factor + offset)

        def one_row(f, r, keep):
            y = act(raw[f, r].astype(F32))
            left = jnp.where(left_ok, act(col[0, f, r]), 0.0)
            right = jnp.where(right_ok, act(col[1, f, r]), 0.0)
            even, odd = y[:across], y[across:]
            planes = (
                jnp.where(row_in == 0, left, pltpu.roll(odd, 1, 0)),
                even,
                odd,
                jnp.where(row_in == across - 1, right, pltpu.roll(even, across - 1, 0)),
            )
            for k, plane in enumerate(planes):
                if keep is not None:
                    plane = jnp.where(keep, plane, 0.0)
                conv_in[k, f, r] = plane.astype(BF16)

        def fill(rows, is_row):
            here = [c for c in copies if is_row(c[0][1])]
            received([c for c in here if c[0][0] == 0])

            @pl.loop(2, 2 + frames)
            def _(f):
                for r, keep in rows:
                    one_row(f, r, keep)

            @pl.when(ta == 0)
            def _():
                for k in range(4):
                    for f in range(2):
                        for r, _ in rows:
                            conv_in[k, f, r] = conv_in[k, 2, r]

            received([c for c in here if c[0][0] == 1])

            @pl.when(ta > 0)
            def _():
                @pl.loop(0, 2)
                def _(f):
                    for r, keep in rows:
                        one_row(f, r, keep)

        def taps(dy, total):
            for dt in range(3):
                window = jnp.concatenate(
                    [
                        conv_in[dx : dx + 2, dt : dt + frames, dy : dy + out_h].reshape(-1, c2)
                        for dx in range(3)
                    ],
                    axis=1,
                )
                part = jnp.dot(
                    window, w[dt, dy].reshape(3 * c2, c2), preferred_element_type=F32
                )
                total = part if total is None else total + part
            return total

        fill([(r, None) for r in range(1, out_h + 1)], lambda dha: dha == 0)
        w_copy.wait()
        acc[...] = taps(1, None)
        fill([(0, above_ok), (out_h + 1, below_ok)], lambda dha: dha != 0)
        total = taps(2, taps(0, acc[...]))
        return total.reshape(2, frames, out_h, across, c2), copies

    hidden, copies2 = norm_conv(1, raw2, col2, stage2, st2, g2, s2, ca_w, fetches[8])
    for b in range(2):
        raw3[2 : 2 + frames, 1 : 1 + out_h, b * across : (b + 1) * across, :] = hidden[b].astype(
            BF16
        )
    branch, copies3 = norm_conv(2, raw3, col3, stage3, st3, g3, s3, cb_w, fetches[9])
    for b in range(2):
        lift = raw2[2 : 2 + frames, 1 : 1 + out_h, b * across : (b + 1) * across, :]
        total = lift.astype(F32) + branch[b]
        for k in range(c2 // 128):
            merged[k, :, :, pl.ds(b, across, stride=2), :] = total[..., k * 128 : (k + 1) * 128]
    for k in range(c2 // 128):
        out[:, :, :, k * 128 : (k + 1) * 128] = merged[k].astype(BF16)

    sent(lat_copies)
    sent(copies2)
    sent(copies3)
    for i, st in enumerate((st1, st2, st3)):
        all_stats(st, i, stat_send)


def per_device(sizes, lat, g1, s1, up_w, g2, s2, ca, g3, s3, cb):
    frames, height, across, c1 = lat.shape
    c2 = up_w.shape[-1]
    out_h, out_w = 2 * height, 2 * across
    n_all = sizes[0] * sizes[1] * sizes[2]
    vmem = pl.BlockSpec(memory_space=pltpu.VMEM)
    hbm = pl.BlockSpec(memory_space=pltpu.HBM)
    field = pltpu.VMEM((frames + 2, out_h + 2, out_w, c2), BF16)
    column = pltpu.VMEM((2, frames + 2, out_h + 2, 1, c2), F32)
    staged = pltpu.VMEM((2, frames, out_h, 1, c2), F32)
    macs = frames * out_h * out_w * 54 * c2 * c2 + frames * height * across * 9 * c1 * c2
    operands = [lat, g1[None], s1[None], up_w, g2[None], s2[None], ca, g3[None], s3[None], cb]
    operands = [pltpu.with_memory_space_constraint(x, pltpu.HBM) for x in operands]
    return pl.pallas_call(
        functools.partial(kernel, sizes),
        out_shape=jax.ShapeDtypeStruct((frames, out_h, out_w, c2), BF16),
        in_specs=[hbm] * 10,
        out_specs=vmem,
        scratch_shapes=[
            pltpu.VMEM(lat.shape, BF16),
            pltpu.VMEM((1, c1), F32),
            pltpu.VMEM((1, c1), F32),
            pltpu.VMEM(up_w.shape, BF16),
            pltpu.VMEM((1, c2), F32),
            pltpu.VMEM((1, c2), F32),
            pltpu.VMEM(ca.shape, BF16),
            pltpu.VMEM((1, c2), F32),
            pltpu.VMEM((1, c2), F32),
            pltpu.VMEM(cb.shape, BF16),
            pltpu.VMEM((frames, across, c1), BF16),
            pltpu.VMEM((frames, height + 1, 1, c1), F32),
            pltpu.VMEM((frames, height, 1, c1), F32),
            pltpu.VMEM((frames, height + 1, across, 2 * c1), BF16),
            field,
            field,
            column,
            column,
            staged,
            staged,
            pltpu.VMEM((4, frames + 2, out_h + 2, across, c2), BF16),
            pltpu.VMEM((frames * out_h * out_w, c2), F32),
            pltpu.VMEM((c2 // 128, frames, out_h, out_w, 128), F32),
            pltpu.VMEM((n_all, 2, c1), F32),
            pltpu.VMEM((n_all, 2, c2), F32),
            pltpu.VMEM((n_all, 2, c2), F32),
            pltpu.SemaphoreType.DMA((10,)),
            pltpu.SemaphoreType.DMA((3, 18)),
            pltpu.SemaphoreType.DMA((3, 18)),
            pltpu.SemaphoreType.DMA((3,)),
            pltpu.SemaphoreType.DMA((3,)),
        ],
        compiler_params=pltpu.CompilerParams(
            collective_id=0, has_side_effects=True, vmem_limit_bytes=44 * 2**20
        ),
        cost_estimate=pl.CostEstimate(
            flops=2 * macs, bytes_accessed=10_000_000, transcendentals=2_000_000
        ),
    )(*operands)


def solution(mesh):
    sizes = (mesh.shape["ha"], mesh.shape["wa"], mesh.shape["ta"])
    fields = P(("videos", "ta"), "ha", "wa", None)
    return jax.shard_map(
        functools.partial(per_device, sizes),
        mesh=mesh,
        in_specs=(fields,) + (P(),) * 9,
        out_specs=fields,
        check_vma=False,
    )
```

```python
import functools
import jax
import jax.numpy as jnp
from jax import lax
from jax.experimental import pallas as pl
from jax.experimental.pallas import tpu as pltpu
from jax.sharding import PartitionSpec as P

GROUPS = 32
EPSILON = 1e-06
MESH = pl.DeviceIdType.MESH
F32 = jnp.float32
BF16 = jnp.bfloat16


def group_moments(mean, squares, count, width):
    means, totals = [], []
    for k in range(mean.shape[1] // 128):
        m, q = (v[:, k * 128 : (k + 1) * 128] for v in (mean, squares))
        lane = lax.broadcasted_iota(jnp.int32, m.shape, 1)
        step = 1
        while step < width:
            low = (lane & step) == 0
            m_other, q_other = (
                jnp.where(low, pltpu.roll(v, 128 - step, 1), pltpu.roll(v, step, 1)) for v in (m, q)
            )
            gap = m - m_other
            q = q + q_other + gap * gap * (0.5 * count * step)
            m = 0.5 * (m + m_other)
            step *= 2
        means.append(m)
        totals.append(q)
    return jnp.concatenate(means, axis=1), jnp.concatenate(totals, axis=1)


def half_silu(h):
    return h + h * jnp.tanh(h)


def kernel(
    sizes,
    lat_hbm,
    g1_hbm,
    s1_hbm,
    up_hbm,
    g2_hbm,
    s2_hbm,
    ca_hbm,
    g3_hbm,
    s3_hbm,
    cb_hbm,
    out,
    lat,
    g1,
    s1,
    up_w,
    g2,
    s2,
    ca_w,
    g3,
    s3,
    cb_w,
    lat_row,
    lat_col,
    lat_stage,
    up_in,
    raw2,
    raw3,
    col2,
    col3,
    stage2,
    stage3,
    conv_in,
    acc,
    merged,
    st1,
    st2,
    st3,
    w_sem,
    halo_send,
    halo_recv,
    stat_send,
    stat_recv,
):
    n_ha, n_wa, n_ta = sizes
    n_all = n_ha * n_wa * n_ta
    ha, wa, ta = lax.axis_index("ha"), lax.axis_index("wa"), lax.axis_index("ta")
    frames, height, across, c1 = lat.shape
    c2 = up_w.shape[-1]
    out_h, out_w = 2 * height, 2 * across

    sources = (lat_hbm, up_hbm, g1_hbm, s1_hbm, g2_hbm, s2_hbm, g3_hbm, s3_hbm, ca_hbm, cb_hbm)
    places = (lat, up_w, g1, s1, g2, s2, g3, s3, ca_w, cb_w)
    fetches = [
        pltpu.make_async_copy(a, b, w_sem.at[i]) for i, (a, b) in enumerate(zip(sources, places))
    ]
    fetches[0].start()
    for fetch in fetches[2:8]:
        fetch.start()

    at_ha = [ha if d == 0 else lax.rem(ha + d, n_ha) for d in range(n_ha)]
    at_wa = [wa if d == 0 else lax.rem(wa + d, n_wa) for d in range(n_wa)]
    at_ta = [ta if d == 0 else lax.rem(ta + d, n_ta) for d in range(n_ta)]

    def peers():
        for slot in range(n_all - 1, 0, -1):
            h, w, t = slot // (n_wa * n_ta), slot // n_ta % n_wa, slot % n_ta
            yield slot, {"ha": at_ha[h], "wa": at_wa[w], "ta": at_ta[t]}

    barrier = pltpu.get_barrier_semaphore()
    for _, device in peers():
        pl.semaphore_signal(barrier, inc=1, device_id=device, device_id_type=MESH)

    def set_stats(st, x):
        rows = x.shape[0]
        mean = jnp.sum(x, axis=0, keepdims=True) * (1.0 / rows)
        centred = x - mean
        st[0, 0:1, :] = mean
        st[0, 1:2, :] = jnp.sum(centred * centred, axis=0, keepdims=True)

    def send_stats(st, i):
        for slot, device in peers():
            pltpu.make_async_remote_copy(
                src_ref=st.at[0],
                dst_ref=st.at[slot],
                send_sem=stat_send.at[i],
                recv_sem=stat_recv.at[i],
                device_id=device,
                device_id_type=MESH,
            ).start()

    def all_stats(st, i, sem):
        pltpu.make_async_copy(st.at[1:n_all], st.at[1:n_all], sem.at[i]).wait()

    def affine(st, i, rows, gain, shift):
        all_stats(st, i, stat_recv)
        c = st.shape[-1]
        width = c // GROUPS
        v = st[...]
        mean_c = jnp.sum(v, axis=0) * (1.0 / n_all)
        kind = lax.broadcasted_iota(jnp.int32, v.shape, 1)
        off = v - mean_c[0:1][None]
        parts = jnp.sum(jnp.where(kind == 0, off * off * float(rows), v), axis=0)
        mean, squares = group_moments(
            jnp.broadcast_to(mean_c[0:1], (8, c)),
            jnp.broadcast_to(parts[0:1] + parts[1:2], (8, c)),
            float(rows * n_all),
            width,
        )
        spread = squares * (1.0 / (width * rows * n_all))
        scaling = lax.rsqrt(spread + EPSILON)
        factor = 0.5 * scaling[0:1] * gain[...]
        return mean[0:1], factor, 0.5 * shift[...]

    def inside(dta, dha, dwa):
        h, w, t = ha + dha, wa + dwa, ta + dta
        ok = (h >= 0) & (h < n_ha) & (w >= 0) & (w < n_wa)
        return ok & (t >= 0) & (t < n_ta)

    def neighbour(dta, dha, dwa):
        return {"ha": ha + dha, "wa": wa + dwa, "ta": ta + dta}

    def remote(src, dst, i, move):
        dta, dha, dwa = move
        k = dta * 9 + (dha + 1) * 3 + dwa + 1
        return pltpu.make_async_remote_copy(
            src_ref=src,
            dst_ref=dst,
            send_sem=halo_send.at[i, k],
            recv_sem=halo_recv.at[i, k],
            device_id=neighbour(*move),
            device_id_type=MESH,
        )

    def start(copies):
        for move, copy in copies:
            pl.when(inside(*move))(copy.start)

    def sent(copies):
        for move, copy in copies:
            pl.when(inside(*move))(copy.wait_send)

    def received(copies):
        for move, copy in copies:
            dta, dha, dwa = move
            pl.when(inside(-dta, -dha, -dwa))(copy.wait_recv)

    def field_copies(i, raw, col, stage, dta):
        copies = []
        f_from, f_to, count = (0, 2, frames) if dta == 0 else (frames - 2, 0, 2)
        for dha in (-1, 0, 1):
            r_from, r_to, n_r = {-1: (0, out_h + 1, 1), 0: (0, 1, out_h), 1: (out_h - 1, 0, 1)}[dha]
            for dwa in (0, -1, 1):
                move = (dta, dha, dwa)
                if move == (0, 0, 0):
                    continue
                fd, rd = pl.ds(f_to, count), pl.ds(r_to, n_r)
                if dwa == 0:
                    src = raw.at[pl.ds(f_from + 2, count), pl.ds(r_from + 1, n_r)]
                    dst = raw.at[fd, rd]
                else:
                    side = (dwa + 1) // 2
                    src = stage.at[side, pl.ds(f_from, count), pl.ds(r_from, n_r)]
                    dst = col.at[1 - side, fd, rd]
                copies.append((move, remote(src, dst, i, move)))
        return copies

    fetches[0].wait()
    for i in (1, 8, 9):
        fetches[i].start()
    set_stats(st1, lat[...].astype(F32).reshape(-1, c1))
    for f in range(frames):
        for r in range(height):
            lat_stage[f, r] = lat[f, r, 0:16, :].astype(F32)[0:1]
    pl.semaphore_wait(barrier, n_all - 1)
    send_stats(st1, 0)
    lat_copies = [
        ((0, -1, 0), remote(lat.at[:, 0], lat_row, 0, (0, -1, 0))),
        ((0, 0, -1), remote(lat_stage, lat_col.at[:, pl.ds(0, height)], 0, (0, 0, -1))),
        (
            (0, -1, -1),
            remote(
                lat_stage.at[:, pl.ds(0, 1)], lat_col.at[:, pl.ds(height, 1)], 0, (0, -1, -1)
            ),
        ),
    ]
    start(lat_copies)
    for fetch in fetches[2:8]:
        fetch.wait()
    mean, factor, offset = affine(st1, 0, frames * height * across, g1, s1)
    received(lat_copies)
    row_in = lax.broadcasted_iota(jnp.int32, (across, 1), 0)
    right_ok, left_ok = wa < n_wa - 1, wa > 0
    below_ok, above_ok = ha < n_ha - 1, ha > 0

    def up_row(f, r, x, keep):
        y = half_silu((x - mean) * factor + offset)
        edge = half_silu((lat_col[f, r] - mean) * factor + offset)
        edge = jnp.where(right_ok, edge, 0.0)
        moved = jnp.where(row_in == across - 1, edge, pltpu.roll(y, across - 1, 0))
        if keep is not None:
            y, moved = jnp.where(keep, y, 0.0), jnp.where(keep, moved, 0.0)
        up_in[f, r, :, 0:c1] = y.astype(BF16)
        up_in[f, r, :, c1 : 2 * c1] = moved.astype(BF16)

    @pl.loop(0, frames)
    def _(f):
        for r in range(height):
            up_row(f, r, lat[f, r].astype(F32), None)
        up_row(f, height, lat_row[f].astype(F32), below_ok)

    fetches[1].wait()

    def tap(dy, dx, ky, kx):
        a = up_in[:, dy : dy + height, :, dx * c1 : (dx + 1) * c1].reshape(-1, c1)
        return jnp.dot(a, up_w[ky, kx], preferred_element_type=F32)

    lifted = {
        (0, 0): lambda: tap(0, 0, 1, 1),
        (0, 1): lambda: tap(0, 0, 1, 2) + tap(0, 1, 1, 0),
        (1, 0): lambda: tap(0, 0, 2, 1) + tap(1, 0, 0, 1),
        (1, 1): lambda: tap(0, 0, 2, 2) + tap(0, 1, 2, 0) + tap(1, 0, 0, 2) + tap(1, 1, 0, 0),
    }
    for (a, b), make in lifted.items():
        block = make().astype(BF16).reshape(frames, height, across, c2)
        for i in range(height):
            raw2[2 : 2 + frames, 1 + 2 * i + a, b * across : (b + 1) * across, :] = block[:, i]

    def norm_conv(i, raw, col, stage, st, gain, shift, w, w_copy):
        own = raw[2 : 2 + frames, 1 : 1 + out_h].astype(F32)
        set_stats(st, own.reshape(-1, c2))
        send_stats(st, i)
        copies = field_copies(i, raw, col, stage, 1) + field_copies(i, raw, col, stage, 0)
        start([c for c in copies if c[0] == (1, 0, 0)])
        for f in range(frames):
            for r in range(out_h):
                stage[0, f, r] = raw[2 + f, 1 + r, 0:16, :].astype(F32)[0:1]
                stage[1, f, r] = raw[2 + f, 1 + r, out_w - 16 : out_w, :].astype(F32)[15:16]
        start([c for c in copies if c[0][2] != 0 and c[0][1] == 0])
        start([c for c in copies if c[0][1] != 0])
        mean, factor, offset = affine(st, i, frames * out_h * out_w, gain, shift)

        def act(x):
            return half_silu((x - mean) * factor + offset)

        def one_row(f, r, keep):
            y = act(raw[f, r].astype(F32))
            left = jnp.where(left_ok, act(col[0, f, r]), 0.0)
            right = jnp.where(right_ok, act(col[1, f, r]), 0.0)
            even, odd = y[:across], y[across:]
            planes = (
                jnp.where(row_in == 0, left, pltpu.roll(odd, 1, 0)),
                even,
                odd,
                jnp.where(row_in == across - 1, right, pltpu.roll(even, across - 1, 0)),
            )
            for k, plane in enumerate(planes):
                if keep is not None:
                    plane = jnp.where(keep, plane, 0.0)
                conv_in[f, r, :, k * c2 : (k + 1) * c2] = plane.astype(BF16)

        def fill(rows, is_row):
            here = [c for c in copies if is_row(c[0][1])]
            received([c for c in here if c[0][0] == 0])

            @pl.loop(2, 2 + frames)
            def _(f):
                for r, keep in rows:
                    one_row(f, r, keep)

            @pl.when(ta == 0)
            def _():
                for f in range(2):
                    for r, _ in rows:
                        conv_in[f, r] = conv_in[2, r]

            received([c for c in here if c[0][0] == 1])

            @pl.when(ta > 0)
            def _():
                @pl.loop(0, 2)
                def _(f):
                    for r, keep in rows:
                        one_row(f, r, keep)

        def taps(b, dy, total):
            for dt in range(3):
                window = conv_in[dt : dt + frames, dy : dy + out_h, :, b * c2 : (b + 3) * c2]
                part = jnp.dot(
                    window.reshape(-1, 3 * c2),
                    w[dt, dy].reshape(3 * c2, c2),
                    preferred_element_type=F32,
                )
                total = part if total is None else total + part
            return total

        fill([(r, None) for r in range(1, out_h + 1)], lambda dha: dha == 0)
        w_copy.wait()
        for b in range(2):
            acc[b] = taps(b, 1, None)
        fill([(0, above_ok), (out_h + 1, below_ok)], lambda dha: dha != 0)
        totals = [taps(b, 2, taps(b, 0, acc[b])) for b in range(2)]
        return [total.reshape(frames, out_h, across, c2) for total in totals], copies

    hidden, copies2 = norm_conv(1, raw2, col2, stage2, st2, g2, s2, ca_w, fetches[8])
    for b in range(2):
        raw3[2 : 2 + frames, 1 : 1 + out_h, b * across : (b + 1) * across, :] = hidden[b].astype(
            BF16
        )
    branch, copies3 = norm_conv(2, raw3, col3, stage3, st3, g3, s3, cb_w, fetches[9])
    for b in range(2):
        lift = raw2[2 : 2 + frames, 1 : 1 + out_h, b * across : (b + 1) * across, :]
        total = lift.astype(F32) + branch[b]
        for k in range(c2 // 128):
            merged[k, :, :, pl.ds(b, across, stride=2), :] = total[..., k * 128 : (k + 1) * 128]
    for k in range(c2 // 128):
        out[:, :, :, k * 128 : (k + 1) * 128] = merged[k].astype(BF16)

    sent(lat_copies)
    sent(copies2)
    sent(copies3)
    for i, st in enumerate((st1, st2, st3)):
        all_stats(st, i, stat_send)


def per_device(sizes, lat, g1, s1, up_w, g2, s2, ca, g3, s3, cb):
    frames, height, across, c1 = lat.shape
    c2 = up_w.shape[-1]
    out_h, out_w = 2 * height, 2 * across
    n_all = sizes[0] * sizes[1] * sizes[2]
    vmem = pl.BlockSpec(memory_space=pltpu.VMEM)
    hbm = pl.BlockSpec(memory_space=pltpu.HBM)
    field = pltpu.VMEM((frames + 2, out_h + 2, out_w, c2), BF16)
    column = pltpu.VMEM((2, frames + 2, out_h + 2, 1, c2), F32)
    staged = pltpu.VMEM((2, frames, out_h, 1, c2), F32)
    macs = frames * out_h * out_w * 54 * c2 * c2 + frames * height * across * 9 * c1 * c2
    operands = [lat, g1[None], s1[None], up_w, g2[None], s2[None], ca, g3[None], s3[None], cb]
    operands = [pltpu.with_memory_space_constraint(x, pltpu.HBM) for x in operands]
    return pl.pallas_call(
        functools.partial(kernel, sizes),
        out_shape=jax.ShapeDtypeStruct((frames, out_h, out_w, c2), BF16),
        in_specs=[hbm] * 10,
        out_specs=vmem,
        scratch_shapes=[
            pltpu.VMEM(lat.shape, BF16),
            pltpu.VMEM((1, c1), F32),
            pltpu.VMEM((1, c1), F32),
            pltpu.VMEM(up_w.shape, BF16),
            pltpu.VMEM((1, c2), F32),
            pltpu.VMEM((1, c2), F32),
            pltpu.VMEM(ca.shape, BF16),
            pltpu.VMEM((1, c2), F32),
            pltpu.VMEM((1, c2), F32),
            pltpu.VMEM(cb.shape, BF16),
            pltpu.VMEM((frames, across, c1), BF16),
            pltpu.VMEM((frames, height + 1, 1, c1), F32),
            pltpu.VMEM((frames, height, 1, c1), F32),
            pltpu.VMEM((frames, height + 1, across, 2 * c1), BF16),
            field,
            field,
            column,
            column,
            staged,
            staged,
            pltpu.VMEM((frames + 2, out_h + 2, across, 4 * c2), BF16),
            pltpu.VMEM((2, frames * out_h * across, c2), F32),
            pltpu.VMEM((c2 // 128, frames, out_h, out_w, 128), F32),
            pltpu.VMEM((n_all, 2, c1), F32),
            pltpu.VMEM((n_all, 2, c2), F32),
            pltpu.VMEM((n_all, 2, c2), F32),
            pltpu.SemaphoreType.DMA((10,)),
            pltpu.SemaphoreType.DMA((3, 18)),
            pltpu.SemaphoreType.DMA((3, 18)),
            pltpu.SemaphoreType.DMA((3,)),
            pltpu.SemaphoreType.DMA((3,)),
        ],
        compiler_params=pltpu.CompilerParams(
            collective_id=0, has_side_effects=True, vmem_limit_bytes=44 * 2**20
        ),
        cost_estimate=pl.CostEstimate(
            flops=2 * macs, bytes_accessed=10_000_000, transcendentals=2_000_000
        ),
    )(*operands)


def solution(mesh):
    sizes = (mesh.shape["ha"], mesh.shape["wa"], mesh.shape["ta"])
    fields = P(("videos", "ta"), "ha", "wa", None)
    return jax.shard_map(
        functools.partial(per_device, sizes),
        mesh=mesh,
        in_specs=(fields,) + (P(),) * 9,
        out_specs=fields,
        check_vma=False,
    )
```

```python
import functools
import jax
import jax.numpy as jnp
from jax import lax
from jax.experimental import pallas as pl
from jax.experimental.pallas import tpu as pltpu
from jax.sharding import PartitionSpec as P

GROUPS = 32
EPSILON = 1e-06
MESH = pl.DeviceIdType.MESH
F32 = jnp.float32
BF16 = jnp.bfloat16


def group_moments(mean, squares, count, width):
    means, totals = [], []
    for k in range(mean.shape[1] // 128):
        m, q = (v[:, k * 128 : (k + 1) * 128] for v in (mean, squares))
        lane = lax.broadcasted_iota(jnp.int32, m.shape, 1)
        step = 1
        while step < width:
            low = (lane & step) == 0
            m_other, q_other = (
                jnp.where(low, pltpu.roll(v, 128 - step, 1), pltpu.roll(v, step, 1)) for v in (m, q)
            )
            gap = m - m_other
            q = q + q_other + gap * gap * (0.5 * count * step)
            m = 0.5 * (m + m_other)
            step *= 2
        means.append(m)
        totals.append(q)
    return jnp.concatenate(means, axis=1), jnp.concatenate(totals, axis=1)


def half_silu(h):
    return h + h * jnp.tanh(h)


def kernel(
    sizes,
    lat_hbm,
    g1_hbm,
    s1_hbm,
    up_hbm,
    g2_hbm,
    s2_hbm,
    ca_hbm,
    g3_hbm,
    s3_hbm,
    cb_hbm,
    out,
    lat,
    g1,
    s1,
    up_w,
    g2,
    s2,
    ca_w,
    g3,
    s3,
    cb_w,
    lat_row,
    lat_col,
    lat_stage,
    up_in,
    raw2,
    raw3,
    col2,
    col3,
    stage2,
    stage3,
    conv_in,
    acc,
    merged,
    st1,
    st2,
    st3,
    w_sem,
    halo_send,
    halo_recv,
    stat_send,
    stat_recv,
):
    n_ha, n_wa, n_ta = sizes
    n_all = n_ha * n_wa * n_ta
    ha, wa, ta = lax.axis_index("ha"), lax.axis_index("wa"), lax.axis_index("ta")
    frames, height, across, c1 = lat.shape
    c2 = up_w.shape[-1]
    out_h, out_w = 2 * height, 2 * across

    sources = (lat_hbm, up_hbm, g1_hbm, s1_hbm, g2_hbm, s2_hbm, g3_hbm, s3_hbm, ca_hbm, cb_hbm)
    places = (lat, up_w, g1, s1, g2, s2, g3, s3, ca_w, cb_w)
    fetches = [
        pltpu.make_async_copy(a, b, w_sem.at[i]) for i, (a, b) in enumerate(zip(sources, places))
    ]
    fetches[0].start()
    for fetch in fetches[2:8]:
        fetch.start()

    at_ha = [ha if d == 0 else lax.rem(ha + d, n_ha) for d in range(n_ha)]
    at_wa = [wa if d == 0 else lax.rem(wa + d, n_wa) for d in range(n_wa)]
    at_ta = [ta if d == 0 else lax.rem(ta + d, n_ta) for d in range(n_ta)]

    def peers():
        for slot in range(n_all - 1, 0, -1):
            h, w, t = slot // (n_wa * n_ta), slot // n_ta % n_wa, slot % n_ta
            yield slot, {"ha": at_ha[h], "wa": at_wa[w], "ta": at_ta[t]}

    barrier = pltpu.get_barrier_semaphore()
    for _, device in peers():
        pl.semaphore_signal(barrier, inc=1, device_id=device, device_id_type=MESH)

    def set_stats(st, x):
        rows = x.shape[0]
        mean = jnp.sum(x, axis=0, keepdims=True) * (1.0 / rows)
        centred = x - mean
        st[0, 0:1, :] = mean
        st[0, 1:2, :] = jnp.sum(centred * centred, axis=0, keepdims=True)

    def send_stats(st, i):
        for slot, device in peers():
            pltpu.make_async_remote_copy(
                src_ref=st.at[0],
                dst_ref=st.at[slot],
                send_sem=stat_send.at[i],
                recv_sem=stat_recv.at[i],
                device_id=device,
                device_id_type=MESH,
            ).start()

    def all_stats(st, i, sem):
        pltpu.make_async_copy(st.at[1:n_all], st.at[1:n_all], sem.at[i]).wait()

    def affine(st, i, rows, gain, shift):
        all_stats(st, i, stat_recv)
        c = st.shape[-1]
        width = c // GROUPS
        v = st[...]
        mean_c = jnp.sum(v, axis=0) * (1.0 / n_all)
        kind = lax.broadcasted_iota(jnp.int32, v.shape, 1)
        off = v - mean_c[0:1][None]
        parts = jnp.sum(jnp.where(kind == 0, off * off * float(rows), v), axis=0)
        mean, squares = group_moments(
            jnp.broadcast_to(mean_c[0:1], (8, c)),
            jnp.broadcast_to(parts[0:1] + parts[1:2], (8, c)),
            float(rows * n_all),
            width,
        )
        spread = squares * (1.0 / (width * rows * n_all))
        scaling = lax.rsqrt(spread + EPSILON)
        factor = 0.5 * scaling[0:1] * gain[...]
        return mean[0:1], factor, 0.5 * shift[...]

    def inside(dta, dha, dwa):
        h, w, t = ha + dha, wa + dwa, ta + dta
        ok = (h >= 0) & (h < n_ha) & (w >= 0) & (w < n_wa)
        return ok & (t >= 0) & (t < n_ta)

    def neighbour(dta, dha, dwa):
        return {"ha": ha + dha, "wa": wa + dwa, "ta": ta + dta}

    def remote(src, dst, i, move):
        dta, dha, dwa = move
        k = dta * 9 + (dha + 1) * 3 + dwa + 1
        return pltpu.make_async_remote_copy(
            src_ref=src,
            dst_ref=dst,
            send_sem=halo_send.at[i, k],
            recv_sem=halo_recv.at[i, k],
            device_id=neighbour(*move),
            device_id_type=MESH,
        )

    def start(copies):
        for move, copy in copies:
            pl.when(inside(*move))(copy.start)

    def sent(copies):
        for move, copy in copies:
            pl.when(inside(*move))(copy.wait_send)

    def received(copies):
        for move, copy in copies:
            dta, dha, dwa = move
            pl.when(inside(-dta, -dha, -dwa))(copy.wait_recv)

    def field_copies(i, raw, col, stage, dta):
        copies = []
        f_from, f_to, count = (0, 2, frames) if dta == 0 else (frames - 2, 0, 2)
        for dha in (-1, 0, 1):
            r_from, r_to, n_r = {-1: (0, out_h + 1, 1), 0: (0, 1, out_h), 1: (out_h - 1, 0, 1)}[dha]
            for dwa in (0, -1, 1):
                move = (dta, dha, dwa)
                if move == (0, 0, 0):
                    continue
                fd, rd = pl.ds(f_to, count), pl.ds(r_to, n_r)
                if dwa == 0:
                    src = raw.at[pl.ds(f_from + 2, count), pl.ds(r_from + 1, n_r)]
                    dst = raw.at[fd, rd]
                else:
                    side = (dwa + 1) // 2
                    src = stage.at[side, pl.ds(f_from, count), pl.ds(r_from, n_r)]
                    dst = col.at[1 - side, fd, rd]
                copies.append((move, remote(src, dst, i, move)))
        return copies

    fetches[0].wait()
    for i in (1, 8, 9):
        fetches[i].start()
    set_stats(st1, lat[...].astype(F32).reshape(-1, c1))
    for f in range(frames):
        for r in range(height):
            lat_stage[f, r] = lat[f, r, 0:16, :].astype(F32)[0:1]
    pl.semaphore_wait(barrier, n_all - 1)
    send_stats(st1, 0)
    lat_copies = [
        ((0, -1, 0), remote(lat.at[:, 0], lat_row, 0, (0, -1, 0))),
        ((0, 0, -1), remote(lat_stage, lat_col.at[:, pl.ds(0, height)], 0, (0, 0, -1))),
        (
            (0, -1, -1),
            remote(
                lat_stage.at[:, pl.ds(0, 1)], lat_col.at[:, pl.ds(height, 1)], 0, (0, -1, -1)
            ),
        ),
    ]
    start(lat_copies)
    for fetch in fetches[2:8]:
        fetch.wait()
    mean, factor, offset = affine(st1, 0, frames * height * across, g1, s1)
    received(lat_copies)
    row_in = lax.broadcasted_iota(jnp.int32, (across, 1), 0)
    right_ok, left_ok = wa < n_wa - 1, wa > 0
    below_ok, above_ok = ha < n_ha - 1, ha > 0

    def up_row(f, r, x, keep):
        y = half_silu((x - mean) * factor + offset)
        edge = half_silu((lat_col[f, r] - mean) * factor + offset)
        edge = jnp.where(right_ok, edge, 0.0)
        moved = jnp.where(row_in == across - 1, edge, pltpu.roll(y, across - 1, 0))
        if keep is not None:
            y, moved = jnp.where(keep, y, 0.0), jnp.where(keep, moved, 0.0)
        up_in[f, r, :, 0:c1] = y.astype(BF16)
        up_in[f, r, :, c1 : 2 * c1] = moved.astype(BF16)

    @pl.loop(0, frames)
    def _(f):
        for r in range(height):
            up_row(f, r, lat[f, r].astype(F32), None)
        up_row(f, height, lat_row[f].astype(F32), below_ok)

    fetches[1].wait()

    def tap(dy, dx, ky, kx):
        a = up_in[:, dy : dy + height, :, dx * c1 : (dx + 1) * c1].reshape(-1, c1)
        return jnp.dot(a, up_w[ky, kx], preferred_element_type=F32)

    lifted = {
        (0, 0): lambda: tap(0, 0, 1, 1),
        (0, 1): lambda: tap(0, 0, 1, 2) + tap(0, 1, 1, 0),
        (1, 0): lambda: tap(0, 0, 2, 1) + tap(1, 0, 0, 1),
        (1, 1): lambda: tap(0, 0, 2, 2) + tap(0, 1, 2, 0) + tap(1, 0, 0, 2) + tap(1, 1, 0, 0),
    }
    for (a, b), make in lifted.items():
        block = make().astype(BF16).reshape(frames, height, across, c2)
        for i in range(height):
            raw2[2 : 2 + frames, 1 + 2 * i + a, b * across : (b + 1) * across, :] = block[:, i]

    def norm_conv(i, raw, col, stage, st, gain, shift, w, w_copy, finish):
        own = raw[2 : 2 + frames, 1 : 1 + out_h].astype(F32)
        set_stats(st, own.reshape(-1, c2))
        send_stats(st, i)
        copies = field_copies(i, raw, col, stage, 1) + field_copies(i, raw, col, stage, 0)
        start([c for c in copies if c[0] == (1, 0, 0)])
        for f in range(frames):
            for r in range(out_h):
                stage[0, f, r] = raw[2 + f, 1 + r, 0:16, :].astype(F32)[0:1]
                stage[1, f, r] = raw[2 + f, 1 + r, out_w - 16 : out_w, :].astype(F32)[15:16]
        start([c for c in copies if c[0][2] != 0 and c[0][1] == 0])
        start([c for c in copies if c[0][1] != 0])
        mean, factor, offset = affine(st, i, frames * out_h * out_w, gain, shift)

        def act(x):
            return half_silu((x - mean) * factor + offset)

        def one_row(f, r, keep):
            y = act(raw[f, r].astype(F32))
            left = jnp.where(left_ok, act(col[0, f, r]), 0.0)
            right = jnp.where(right_ok, act(col[1, f, r]), 0.0)
            even, odd = y[:across], y[across:]
            planes = (
                jnp.where(row_in == 0, left, pltpu.roll(odd, 1, 0)),
                even,
                odd,
                jnp.where(row_in == across - 1, right, pltpu.roll(even, across - 1, 0)),
            )
            for k, plane in enumerate(planes):
                if keep is not None:
                    plane = jnp.where(keep, plane, 0.0)
                conv_in[f, r, :, k * c2 : (k + 1) * c2] = plane.astype(BF16)

        def fill(rows, is_row):
            here = [c for c in copies if is_row(c[0][1])]
            received([c for c in here if c[0][0] == 0])

            @pl.loop(2, 2 + frames)
            def _(f):
                for r, keep in rows:
                    one_row(f, r, keep)

            @pl.when(ta == 0)
            def _():
                for f in range(2):
                    for r, _ in rows:
                        conv_in[f, r] = conv_in[2, r]

            received([c for c in here if c[0][0] == 1])

            @pl.when(ta > 0)
            def _():
                @pl.loop(0, 2)
                def _(f):
                    for r, keep in rows:
                        one_row(f, r, keep)

        def taps(b, f, rows, total):
            for dt in range(3):
                for dy in rows:
                    window = conv_in[f + dt, dy : dy + out_h, :, b * c2 : (b + 3) * c2]
                    part = jnp.dot(
                        window.reshape(-1, 3 * c2),
                        w[dt, dy].reshape(3 * c2, c2),
                        preferred_element_type=F32,
                    )
                    total = part if total is None else total + part
            return total

        fill([(r, None) for r in range(1, out_h + 1)], lambda dha: dha == 0)
        w_copy.wait()
        for b in range(2):
            for f in range(frames):
                acc[b, f] = taps(b, f, (1,), None)
        fill([(0, above_ok), (out_h + 1, below_ok)], lambda dha: dha != 0)
        for b in range(2):
            for f in range(frames):
                finish(b, f, taps(b, f, (0, 2), acc[b, f]).reshape(out_h, across, c2))
        return copies

    def keep_hidden(b, f, hidden):
        raw3[2 + f, 1 : 1 + out_h, b * across : (b + 1) * across, :] = hidden.astype(BF16)

    def merge(b, f, branch):
        lift = raw2[2 + f, 1 : 1 + out_h, b * across : (b + 1) * across, :]
        total = lift.astype(F32) + branch
        for k in range(c2 // 128):
            merged[k, f, :, pl.ds(b, across, stride=2), :] = total[..., k * 128 : (k + 1) * 128]

    copies2 = norm_conv(
        1, raw2, col2, stage2, st2, g2, s2, ca_w, fetches[8], keep_hidden
    )
    copies3 = norm_conv(2, raw3, col3, stage3, st3, g3, s3, cb_w, fetches[9], merge)
    for k in range(c2 // 128):
        out[:, :, :, k * 128 : (k + 1) * 128] = merged[k].astype(BF16)

    sent(lat_copies)
    sent(copies2)
    sent(copies3)
    for i, st in enumerate((st1, st2, st3)):
        all_stats(st, i, stat_send)


def per_device(sizes, lat, g1, s1, up_w, g2, s2, ca, g3, s3, cb):
    frames, height, across, c1 = lat.shape
    c2 = up_w.shape[-1]
    out_h, out_w = 2 * height, 2 * across
    n_all = sizes[0] * sizes[1] * sizes[2]
    vmem = pl.BlockSpec(memory_space=pltpu.VMEM)
    hbm = pl.BlockSpec(memory_space=pltpu.HBM)
    field = pltpu.VMEM((frames + 2, out_h + 2, out_w, c2), BF16)
    column = pltpu.VMEM((2, frames + 2, out_h + 2, 1, c2), F32)
    staged = pltpu.VMEM((2, frames, out_h, 1, c2), F32)
    macs = frames * out_h * out_w * 54 * c2 * c2 + frames * height * across * 9 * c1 * c2
    operands = [lat, g1[None], s1[None], up_w, g2[None], s2[None], ca, g3[None], s3[None], cb]
    operands = [pltpu.with_memory_space_constraint(x, pltpu.HBM) for x in operands]
    return pl.pallas_call(
        functools.partial(kernel, sizes),
        out_shape=jax.ShapeDtypeStruct((frames, out_h, out_w, c2), BF16),
        in_specs=[hbm] * 10,
        out_specs=vmem,
        scratch_shapes=[
            pltpu.VMEM(lat.shape, BF16),
            pltpu.VMEM((1, c1), F32),
            pltpu.VMEM((1, c1), F32),
            pltpu.VMEM(up_w.shape, BF16),
            pltpu.VMEM((1, c2), F32),
            pltpu.VMEM((1, c2), F32),
            pltpu.VMEM(ca.shape, BF16),
            pltpu.VMEM((1, c2), F32),
            pltpu.VMEM((1, c2), F32),
            pltpu.VMEM(cb.shape, BF16),
            pltpu.VMEM((frames, across, c1), BF16),
            pltpu.VMEM((frames, height + 1, 1, c1), F32),
            pltpu.VMEM((frames, height, 1, c1), F32),
            pltpu.VMEM((frames, height + 1, across, 2 * c1), BF16),
            field,
            field,
            column,
            column,
            staged,
            staged,
            pltpu.VMEM((frames + 2, out_h + 2, across, 4 * c2), BF16),
            pltpu.VMEM((2, frames, out_h * across, c2), F32),
            pltpu.VMEM((c2 // 128, frames, out_h, out_w, 128), F32),
            pltpu.VMEM((n_all, 2, c1), F32),
            pltpu.VMEM((n_all, 2, c2), F32),
            pltpu.VMEM((n_all, 2, c2), F32),
            pltpu.SemaphoreType.DMA((10,)),
            pltpu.SemaphoreType.DMA((3, 18)),
            pltpu.SemaphoreType.DMA((3, 18)),
            pltpu.SemaphoreType.DMA((3,)),
            pltpu.SemaphoreType.DMA((3,)),
        ],
        compiler_params=pltpu.CompilerParams(
            collective_id=0, has_side_effects=True, vmem_limit_bytes=44 * 2**20
        ),
        cost_estimate=pl.CostEstimate(
            flops=2 * macs, bytes_accessed=10_000_000, transcendentals=2_000_000
        ),
    )(*operands)


def solution(mesh):
    sizes = (mesh.shape["ha"], mesh.shape["wa"], mesh.shape["ta"])
    fields = P(("videos", "ta"), "ha", "wa", None)
    return jax.shard_map(
        functools.partial(per_device, sizes),
        mesh=mesh,
        in_specs=(fields,) + (P(),) * 9,
        out_specs=fields,
        check_vma=False,
    )
```

```python
import functools
import jax
import jax.numpy as jnp
from jax import lax
from jax.experimental import pallas as pl
from jax.experimental.pallas import tpu as pltpu
from jax.sharding import PartitionSpec as P

GROUPS = 32
EPSILON = 1e-06
MESH = pl.DeviceIdType.MESH
F32 = jnp.float32
BF16 = jnp.bfloat16


def group_moments(mean, squares, count, width):
    means, totals = [], []
    for k in range(mean.shape[1] // 128):
        m, q = (v[:, k * 128 : (k + 1) * 128] for v in (mean, squares))
        lane = lax.broadcasted_iota(jnp.int32, m.shape, 1)
        step = 1
        while step < width:
            low = (lane & step) == 0
            m_other, q_other = (
                jnp.where(low, pltpu.roll(v, 128 - step, 1), pltpu.roll(v, step, 1)) for v in (m, q)
            )
            gap = m - m_other
            q = q + q_other + gap * gap * (0.5 * count * step)
            m = 0.5 * (m + m_other)
            step *= 2
        means.append(m)
        totals.append(q)
    return jnp.concatenate(means, axis=1), jnp.concatenate(totals, axis=1)


def half_silu(h):
    return h + h * jnp.tanh(h)


def kernel(
    sizes,
    lat_hbm,
    g1_hbm,
    s1_hbm,
    up_hbm,
    g2_hbm,
    s2_hbm,
    ca_hbm,
    g3_hbm,
    s3_hbm,
    cb_hbm,
    out,
    lat,
    g1,
    s1,
    up_w,
    g2,
    s2,
    ca_w,
    g3,
    s3,
    cb_w,
    lat_row,
    lat_col,
    lat_stage,
    up_in,
    raw2,
    raw3,
    col2,
    col3,
    stage2,
    stage3,
    conv_in,
    acc,
    merged,
    st1,
    st2,
    st3,
    w_sem,
    halo_send,
    halo_recv,
    stat_send,
    stat_recv,
):
    n_ha, n_wa, n_ta = sizes
    n_all = n_ha * n_wa * n_ta
    ha, wa, ta = lax.axis_index("ha"), lax.axis_index("wa"), lax.axis_index("ta")
    frames, height, across, c1 = lat.shape
    c2 = up_w.shape[-1]
    out_h, out_w = 2 * height, 2 * across

    sources = (lat_hbm, up_hbm, g1_hbm, s1_hbm, g2_hbm, s2_hbm, g3_hbm, s3_hbm, ca_hbm, cb_hbm)
    places = (lat, up_w, g1, s1, g2, s2, g3, s3, ca_w, cb_w)
    fetches = [
        pltpu.make_async_copy(a, b, w_sem.at[i]) for i, (a, b) in enumerate(zip(sources, places))
    ]
    fetches[0].start()
    for fetch in fetches[2:8]:
        fetch.start()

    at_ha = [ha if d == 0 else lax.rem(ha + d, n_ha) for d in range(n_ha)]
    at_wa = [wa if d == 0 else lax.rem(wa + d, n_wa) for d in range(n_wa)]
    at_ta = [ta if d == 0 else lax.rem(ta + d, n_ta) for d in range(n_ta)]

    def peers():
        for slot in range(n_all - 1, 0, -1):
            h, w, t = slot // (n_wa * n_ta), slot // n_ta % n_wa, slot % n_ta
            yield slot, {"ha": at_ha[h], "wa": at_wa[w], "ta": at_ta[t]}

    barrier = pltpu.get_barrier_semaphore()
    for _, device in peers():
        pl.semaphore_signal(barrier, inc=1, device_id=device, device_id_type=MESH)

    def set_stats(st, x):
        rows = x.shape[0]
        mean = jnp.sum(x, axis=0, keepdims=True) * (1.0 / rows)
        centred = x - mean
        st[0, 0:1, :] = mean
        st[0, 1:2, :] = jnp.sum(centred * centred, axis=0, keepdims=True)

    def send_stats(st, i):
        for slot, device in peers():
            pltpu.make_async_remote_copy(
                src_ref=st.at[0],
                dst_ref=st.at[slot],
                send_sem=stat_send.at[i],
                recv_sem=stat_recv.at[i],
                device_id=device,
                device_id_type=MESH,
            ).start()

    def all_stats(st, i, sem):
        pltpu.make_async_copy(st.at[1:n_all], st.at[1:n_all], sem.at[i]).wait()

    def affine(st, i, rows, gain, shift):
        all_stats(st, i, stat_recv)
        c = st.shape[-1]
        width = c // GROUPS
        v = st[...]
        mean_c = jnp.sum(v, axis=0) * (1.0 / n_all)
        kind = lax.broadcasted_iota(jnp.int32, v.shape, 1)
        off = v - mean_c[0:1][None]
        parts = jnp.sum(jnp.where(kind == 0, off * off * float(rows), v), axis=0)
        mean, squares = group_moments(
            jnp.broadcast_to(mean_c[0:1], (8, c)),
            jnp.broadcast_to(parts[0:1] + parts[1:2], (8, c)),
            float(rows * n_all),
            width,
        )
        spread = squares * (1.0 / (width * rows * n_all))
        scaling = lax.rsqrt(spread + EPSILON)
        factor = 0.5 * scaling[0:1] * gain[...]
        return mean[0:1], factor, 0.5 * shift[...]

    def inside(dta, dha, dwa):
        h, w, t = ha + dha, wa + dwa, ta + dta
        ok = (h >= 0) & (h < n_ha) & (w >= 0) & (w < n_wa)
        return ok & (t >= 0) & (t < n_ta)

    def neighbour(dta, dha, dwa):
        return {"ha": ha + dha, "wa": wa + dwa, "ta": ta + dta}

    def remote(src, dst, i, move):
        dta, dha, dwa = move
        k = dta * 9 + (dha + 1) * 3 + dwa + 1
        return pltpu.make_async_remote_copy(
            src_ref=src,
            dst_ref=dst,
            send_sem=halo_send.at[i, k],
            recv_sem=halo_recv.at[i, k],
            device_id=neighbour(*move),
            device_id_type=MESH,
        )

    def start(copies):
        for move, copy in copies:
            pl.when(inside(*move))(copy.start)

    def sent(copies):
        for move, copy in copies:
            pl.when(inside(*move))(copy.wait_send)

    def received(copies):
        for move, copy in copies:
            dta, dha, dwa = move
            pl.when(inside(-dta, -dha, -dwa))(copy.wait_recv)

    def field_copies(i, raw, col, stage, dta):
        copies = []
        f_from, f_to, count = (0, 2, frames) if dta == 0 else (frames - 2, 0, 2)
        for dha in (-1, 0, 1):
            r_from, r_to, n_r = {-1: (0, out_h + 1, 1), 0: (0, 1, out_h), 1: (out_h - 1, 0, 1)}[dha]
            for dwa in (0, -1, 1):
                move = (dta, dha, dwa)
                if move == (0, 0, 0):
                    continue
                fd, rd = pl.ds(f_to, count), pl.ds(r_to, n_r)
                if dwa == 0:
                    src = raw.at[pl.ds(f_from + 2, count), pl.ds(r_from + 1, n_r)]
                    dst = raw.at[fd, rd]
                else:
                    side = (dwa + 1) // 2
                    src = stage.at[side, pl.ds(f_from, count), pl.ds(r_from, n_r)]
                    dst = col.at[1 - side, fd, rd]
                copies.append((move, remote(src, dst, i, move)))
        return copies

    fetches[0].wait()
    for i in (1, 8, 9):
        fetches[i].start()
    set_stats(st1, lat[...].astype(F32).reshape(-1, c1))
    for f in range(frames):
        for r in range(height):
            lat_stage[f, r] = lat[f, r, 0:16, :].astype(F32)[0:1]
    pl.semaphore_wait(barrier, n_all - 1)
    send_stats(st1, 0)
    lat_copies = [
        ((0, -1, 0), remote(lat.at[:, 0], lat_row, 0, (0, -1, 0))),
        ((0, 0, -1), remote(lat_stage, lat_col.at[:, pl.ds(0, height)], 0, (0, 0, -1))),
        (
            (0, -1, -1),
            remote(
                lat_stage.at[:, pl.ds(0, 1)], lat_col.at[:, pl.ds(height, 1)], 0, (0, -1, -1)
            ),
        ),
    ]
    start(lat_copies)
    for fetch in fetches[2:8]:
        fetch.wait()
    mean, factor, offset = affine(st1, 0, frames * height * across, g1, s1)
    received(lat_copies)
    row_in = lax.broadcasted_iota(jnp.int32, (across, 1), 0)
    right_ok, left_ok = wa < n_wa - 1, wa > 0
    below_ok, above_ok = ha < n_ha - 1, ha > 0

    def up_row(f, r, x, keep):
        y = half_silu((x - mean) * factor + offset)
        edge = half_silu((lat_col[f, r] - mean) * factor + offset)
        edge = jnp.where(right_ok, edge, 0.0)
        moved = jnp.where(row_in == across - 1, edge, pltpu.roll(y, across - 1, 0))
        if keep is not None:
            y, moved = jnp.where(keep, y, 0.0), jnp.where(keep, moved, 0.0)
        up_in[f, r, :, 0:c1] = y.astype(BF16)
        up_in[f, r, :, c1 : 2 * c1] = moved.astype(BF16)

    @pl.loop(0, frames)
    def _(f):
        for r in range(height):
            up_row(f, r, lat[f, r].astype(F32), None)
        up_row(f, height, lat_row[f].astype(F32), below_ok)

    fetches[1].wait()

    def tap(dy, dx, ky, kx):
        a = up_in[:, dy : dy + height, :, dx * c1 : (dx + 1) * c1].reshape(-1, c1)
        return jnp.dot(a, up_w[ky, kx], preferred_element_type=F32)

    lifted = {
        (0, 0): lambda: tap(0, 0, 1, 1),
        (0, 1): lambda: tap(0, 0, 1, 2) + tap(0, 1, 1, 0),
        (1, 0): lambda: tap(0, 0, 2, 1) + tap(1, 0, 0, 1),
        (1, 1): lambda: tap(0, 0, 2, 2) + tap(0, 1, 2, 0) + tap(1, 0, 0, 2) + tap(1, 1, 0, 0),
    }
    for (a, b), make in lifted.items():
        block = make().astype(BF16).reshape(frames, height, across, c2)
        for i in range(height):
            raw2[2 : 2 + frames, 1 + 2 * i + a, b * across : (b + 1) * across, :] = block[:, i]

    def norm_conv(i, raw, col, stage, st, gain, shift, w, w_copy):
        own = raw[2 : 2 + frames, 1 : 1 + out_h].astype(F32)
        set_stats(st, own.reshape(-1, c2))
        send_stats(st, i)
        copies = field_copies(i, raw, col, stage, 1) + field_copies(i, raw, col, stage, 0)
        start([c for c in copies if c[0] == (1, 0, 0)])
        for f in range(frames):
            for r in range(out_h):
                stage[0, f, r] = raw[2 + f, 1 + r, 0:16, :].astype(F32)[0:1]
                stage[1, f, r] = raw[2 + f, 1 + r, out_w - 16 : out_w, :].astype(F32)[15:16]
        start([c for c in copies if c[0][2] != 0 and c[0][1] == 0])
        start([c for c in copies if c[0][1] != 0])
        mean, factor, offset = affine(st, i, frames * out_h * out_w, gain, shift)

        def act(x):
            return half_silu((x - mean) * factor + offset)

        def one_row(f, r, keep):
            y = act(raw[f, r].astype(F32))
            left = jnp.where(left_ok, act(col[0, f, r]), 0.0)
            right = jnp.where(right_ok, act(col[1, f, r]), 0.0)
            even, odd = y[:across], y[across:]
            before = jnp.where(row_in == 0, left, pltpu.roll(odd, 1, 0))
            after = jnp.where(row_in == across - 1, right, pltpu.roll(even, across - 1, 0))
            if keep is not None:
                before, even, odd, after = (
                    jnp.where(keep, plane, 0.0) for plane in (before, even, odd, after)
                )
            before, even, odd, after = (p.astype(BF16) for p in (before, even, odd, after))
            for b, planes in enumerate(((before, even, odd), (even, odd, after))):
                for k, plane in enumerate(planes):
                    conv_in[f, r, b * across : (b + 1) * across, k * c2 : (k + 1) * c2] = plane

        def fill(rows, is_row):
            here = [c for c in copies if is_row(c[0][1])]
            received([c for c in here if c[0][0] == 0])

            @pl.loop(2, 2 + frames)
            def _(f):
                for r, keep in rows:
                    one_row(f, r, keep)

            @pl.when(ta == 0)
            def _():
                for f in range(2):
                    for r, _ in rows:
                        conv_in[f, r] = conv_in[2, r]

            received([c for c in here if c[0][0] == 1])

            @pl.when(ta > 0)
            def _():
                @pl.loop(0, 2)
                def _(f):
                    for r, keep in rows:
                        one_row(f, r, keep)

        def taps(dy, total):
            for dt in range(3):
                part = jnp.dot(
                    conv_in[dt : dt + frames, dy : dy + out_h].reshape(-1, 3 * c2),
                    w[dt, dy].reshape(3 * c2, c2),
                    preferred_element_type=F32,
                )
                total = part if total is None else total + part
            return total

        fill([(r, None) for r in range(1, out_h + 1)], lambda dha: dha == 0)
        w_copy.wait()
        acc[...] = taps(1, None)
        fill([(0, above_ok), (out_h + 1, below_ok)], lambda dha: dha != 0)
        total = taps(2, taps(0, acc[...])).reshape(frames, out_h, out_w, c2)
        return [total[:, :, b * across : (b + 1) * across] for b in range(2)], copies

    hidden, copies2 = norm_conv(1, raw2, col2, stage2, st2, g2, s2, ca_w, fetches[8])
    for b in range(2):
        raw3[2 : 2 + frames, 1 : 1 + out_h, b * across : (b + 1) * across, :] = hidden[b].astype(
            BF16
        )
    branch, copies3 = norm_conv(2, raw3, col3, stage3, st3, g3, s3, cb_w, fetches[9])
    for b in range(2):
        lift = raw2[2 : 2 + frames, 1 : 1 + out_h, b * across : (b + 1) * across, :]
        total = lift.astype(F32) + branch[b]
        for k in range(c2 // 128):
            merged[k, :, :, pl.ds(b, across, stride=2), :] = total[..., k * 128 : (k + 1) * 128]
    for k in range(c2 // 128):
        out[:, :, :, k * 128 : (k + 1) * 128] = merged[k].astype(BF16)

    sent(lat_copies)
    sent(copies2)
    sent(copies3)
    for i, st in enumerate((st1, st2, st3)):
        all_stats(st, i, stat_send)


def per_device(sizes, lat, g1, s1, up_w, g2, s2, ca, g3, s3, cb):
    frames, height, across, c1 = lat.shape
    c2 = up_w.shape[-1]
    out_h, out_w = 2 * height, 2 * across
    n_all = sizes[0] * sizes[1] * sizes[2]
    vmem = pl.BlockSpec(memory_space=pltpu.VMEM)
    hbm = pl.BlockSpec(memory_space=pltpu.HBM)
    field = pltpu.VMEM((frames + 2, out_h + 2, out_w, c2), BF16)
    column = pltpu.VMEM((2, frames + 2, out_h + 2, 1, c2), F32)
    staged = pltpu.VMEM((2, frames, out_h, 1, c2), F32)
    macs = frames * out_h * out_w * 54 * c2 * c2 + frames * height * across * 9 * c1 * c2
    operands = [lat, g1[None], s1[None], up_w, g2[None], s2[None], ca, g3[None], s3[None], cb]
    operands = [pltpu.with_memory_space_constraint(x, pltpu.HBM) for x in operands]
    return pl.pallas_call(
        functools.partial(kernel, sizes),
        out_shape=jax.ShapeDtypeStruct((frames, out_h, out_w, c2), BF16),
        in_specs=[hbm] * 10,
        out_specs=vmem,
        scratch_shapes=[
            pltpu.VMEM(lat.shape, BF16),
            pltpu.VMEM((1, c1), F32),
            pltpu.VMEM((1, c1), F32),
            pltpu.VMEM(up_w.shape, BF16),
            pltpu.VMEM((1, c2), F32),
            pltpu.VMEM((1, c2), F32),
            pltpu.VMEM(ca.shape, BF16),
            pltpu.VMEM((1, c2), F32),
            pltpu.VMEM((1, c2), F32),
            pltpu.VMEM(cb.shape, BF16),
            pltpu.VMEM((frames, across, c1), BF16),
            pltpu.VMEM((frames, height + 1, 1, c1), F32),
            pltpu.VMEM((frames, height, 1, c1), F32),
            pltpu.VMEM((frames, height + 1, across, 2 * c1), BF16),
            field,
            field,
            column,
            column,
            staged,
            staged,
            pltpu.VMEM((frames + 2, out_h + 2, out_w, 3 * c2), BF16),
            pltpu.VMEM((frames * out_h * out_w, c2), F32),
            pltpu.VMEM((c2 // 128, frames, out_h, out_w, 128), F32),
            pltpu.VMEM((n_all, 2, c1), F32),
            pltpu.VMEM((n_all, 2, c2), F32),
            pltpu.VMEM((n_all, 2, c2), F32),
            pltpu.SemaphoreType.DMA((10,)),
            pltpu.SemaphoreType.DMA((3, 18)),
            pltpu.SemaphoreType.DMA((3, 18)),
            pltpu.SemaphoreType.DMA((3,)),
            pltpu.SemaphoreType.DMA((3,)),
        ],
        compiler_params=pltpu.CompilerParams(
            collective_id=0, has_side_effects=True, vmem_limit_bytes=44 * 2**20
        ),
        cost_estimate=pl.CostEstimate(
            flops=2 * macs, bytes_accessed=10_000_000, transcendentals=2_000_000
        ),
    )(*operands)


def solution(mesh):
    sizes = (mesh.shape["ha"], mesh.shape["wa"], mesh.shape["ta"])
    fields = P(("videos", "ta"), "ha", "wa", None)
    return jax.shard_map(
        functools.partial(per_device, sizes),
        mesh=mesh,
        in_specs=(fields,) + (P(),) * 9,
        out_specs=fields,
        check_vma=False,
    )
```

```python
import functools
import jax
import jax.numpy as jnp
from jax import lax
from jax.experimental import pallas as pl
from jax.experimental.pallas import tpu as pltpu
from jax.sharding import PartitionSpec as P

GROUPS = 32
EPSILON = 1e-06
MESH = pl.DeviceIdType.MESH
F32 = jnp.float32
BF16 = jnp.bfloat16


def group_moments(mean, squares, count, width):
    means, totals = [], []
    for k in range(mean.shape[1] // 128):
        m, q = (v[:, k * 128 : (k + 1) * 128] for v in (mean, squares))
        lane = lax.broadcasted_iota(jnp.int32, m.shape, 1)
        step = 1
        while step < width:
            low = (lane & step) == 0
            m_other, q_other = (
                jnp.where(low, pltpu.roll(v, 128 - step, 1), pltpu.roll(v, step, 1)) for v in (m, q)
            )
            gap = m - m_other
            q = q + q_other + gap * gap * (0.5 * count * step)
            m = 0.5 * (m + m_other)
            step *= 2
        means.append(m)
        totals.append(q)
    return jnp.concatenate(means, axis=1), jnp.concatenate(totals, axis=1)


def half_silu(h):
    return h + h * jnp.tanh(h)


def kernel(
    sizes,
    lat_hbm,
    g1_hbm,
    s1_hbm,
    up_hbm,
    g2_hbm,
    s2_hbm,
    ca_hbm,
    g3_hbm,
    s3_hbm,
    cb_hbm,
    out,
    lat,
    g1,
    s1,
    up_w,
    g2,
    s2,
    ca_w,
    g3,
    s3,
    cb_w,
    lat_row,
    lat_col,
    lat_stage,
    up_in,
    raw2,
    raw3,
    col2,
    col3,
    stage2,
    stage3,
    conv_in,
    acc,
    merged,
    st1,
    st2,
    st3,
    w_sem,
    halo_send,
    halo_recv,
    stat_send,
    stat_recv,
):
    n_ha, n_wa, n_ta = sizes
    n_all = n_ha * n_wa * n_ta
    ha, wa, ta = lax.axis_index("ha"), lax.axis_index("wa"), lax.axis_index("ta")
    frames, height, across, c1 = lat.shape
    c2 = up_w.shape[-1]
    out_h, out_w = 2 * height, 2 * across

    sources = (lat_hbm, up_hbm, g1_hbm, s1_hbm, g2_hbm, s2_hbm, g3_hbm, s3_hbm, ca_hbm, cb_hbm)
    places = (lat, up_w, g1, s1, g2, s2, g3, s3, ca_w, cb_w)
    fetches = [
        pltpu.make_async_copy(a, b, w_sem.at[i]) for i, (a, b) in enumerate(zip(sources, places))
    ]
    fetches[0].start()
    for fetch in fetches[2:8]:
        fetch.start()

    at_ha = [ha if d == 0 else lax.rem(ha + d, n_ha) for d in range(n_ha)]
    at_wa = [wa if d == 0 else lax.rem(wa + d, n_wa) for d in range(n_wa)]
    at_ta = [ta if d == 0 else lax.rem(ta + d, n_ta) for d in range(n_ta)]

    def peers():
        for slot in range(n_all - 1, 0, -1):
            h, w, t = slot // (n_wa * n_ta), slot // n_ta % n_wa, slot % n_ta
            yield slot, {"ha": at_ha[h], "wa": at_wa[w], "ta": at_ta[t]}

    barrier = pltpu.get_barrier_semaphore()
    for _, device in peers():
        pl.semaphore_signal(barrier, inc=1, device_id=device, device_id_type=MESH)

    def set_stats(st, x):
        rows = x.shape[0]
        mean = jnp.sum(x, axis=0, keepdims=True) * (1.0 / rows)
        centred = x - mean
        st[0, 0:1, :] = mean
        st[0, 1:2, :] = jnp.sum(centred * centred, axis=0, keepdims=True)

    def send_stats(st, i):
        for slot, device in peers():
            pltpu.make_async_remote_copy(
                src_ref=st.at[0],
                dst_ref=st.at[slot],
                send_sem=stat_send.at[i],
                recv_sem=stat_recv.at[i],
                device_id=device,
                device_id_type=MESH,
            ).start()

    def all_stats(st, i, sem):
        pltpu.make_async_copy(st.at[1:n_all], st.at[1:n_all], sem.at[i]).wait()

    def affine(st, i, rows, gain, shift):
        all_stats(st, i, stat_recv)
        c = st.shape[-1]
        width = c // GROUPS
        v = st[...]
        mean_c = jnp.sum(v, axis=0) * (1.0 / n_all)
        kind = lax.broadcasted_iota(jnp.int32, v.shape, 1)
        off = v - mean_c[0:1][None]
        parts = jnp.sum(jnp.where(kind == 0, off * off * float(rows), v), axis=0)
        mean, squares = group_moments(
            jnp.broadcast_to(mean_c[0:1], (8, c)),
            jnp.broadcast_to(parts[0:1] + parts[1:2], (8, c)),
            float(rows * n_all),
            width,
        )
        spread = squares * (1.0 / (width * rows * n_all))
        scaling = lax.rsqrt(spread + EPSILON)
        factor = 0.5 * scaling[0:1] * gain[...]
        return mean[0:1], factor, 0.5 * shift[...]

    def inside(dta, dha, dwa):
        h, w, t = ha + dha, wa + dwa, ta + dta
        ok = (h >= 0) & (h < n_ha) & (w >= 0) & (w < n_wa)
        return ok & (t >= 0) & (t < n_ta)

    def neighbour(dta, dha, dwa):
        return {"ha": ha + dha, "wa": wa + dwa, "ta": ta + dta}

    def remote(src, dst, i, move):
        dta, dha, dwa = move
        k = dta * 9 + (dha + 1) * 3 + dwa + 1
        return pltpu.make_async_remote_copy(
            src_ref=src,
            dst_ref=dst,
            send_sem=halo_send.at[i, k],
            recv_sem=halo_recv.at[i, k],
            device_id=neighbour(*move),
            device_id_type=MESH,
        )

    def start(copies):
        for move, copy in copies:
            pl.when(inside(*move))(copy.start)

    def sent(copies):
        for move, copy in copies:
            pl.when(inside(*move))(copy.wait_send)

    def received(copies):
        for move, copy in copies:
            dta, dha, dwa = move
            pl.when(inside(-dta, -dha, -dwa))(copy.wait_recv)

    def field_copies(i, raw, col, stage, dta):
        copies = []
        f_from, f_to, count = (0, 2, frames) if dta == 0 else (frames - 2, 0, 2)
        for dha in (-1, 0, 1):
            r_from, r_to, n_r = {-1: (0, out_h + 1, 1), 0: (0, 1, out_h), 1: (out_h - 1, 0, 1)}[dha]
            for dwa in (0, -1, 1):
                move = (dta, dha, dwa)
                if move == (0, 0, 0):
                    continue
                fd, rd = pl.ds(f_to, count), pl.ds(r_to, n_r)
                if dwa == 0:
                    src = raw.at[pl.ds(f_from + 2, count), pl.ds(r_from + 1, n_r)]
                    dst = raw.at[fd, rd]
                else:
                    side = (dwa + 1) // 2
                    src = stage.at[side, pl.ds(f_from, count), pl.ds(r_from, n_r)]
                    dst = col.at[1 - side, fd, rd]
                copies.append((move, remote(src, dst, i, move)))
        return copies

    fetches[0].wait()
    for i in (1, 8, 9):
        fetches[i].start()
    set_stats(st1, lat[...].astype(F32).reshape(-1, c1))
    for f in range(frames):
        for r in range(height):
            lat_stage[f, r] = lat[f, r, 0:16, :].astype(F32)[0:1]
    pl.semaphore_wait(barrier, n_all - 1)
    send_stats(st1, 0)
    lat_copies = [
        ((0, -1, 0), remote(lat.at[:, 0], lat_row, 0, (0, -1, 0))),
        ((0, 0, -1), remote(lat_stage, lat_col.at[:, pl.ds(0, height)], 0, (0, 0, -1))),
        (
            (0, -1, -1),
            remote(
                lat_stage.at[:, pl.ds(0, 1)], lat_col.at[:, pl.ds(height, 1)], 0, (0, -1, -1)
            ),
        ),
    ]
    start(lat_copies)
    for fetch in fetches[2:8]:
        fetch.wait()
    mean, factor, offset = affine(st1, 0, frames * height * across, g1, s1)
    received(lat_copies)
    row_in = lax.broadcasted_iota(jnp.int32, (across, 1), 0)
    right_ok, left_ok = wa < n_wa - 1, wa > 0
    below_ok, above_ok = ha < n_ha - 1, ha > 0

    def up_row(f, r, x, keep):
        y = half_silu((x - mean) * factor + offset)
        edge = half_silu((lat_col[f, r] - mean) * factor + offset)
        edge = jnp.where(right_ok, edge, 0.0)
        moved = jnp.where(row_in == across - 1, edge, pltpu.roll(y, across - 1, 0))
        if keep is not None:
            y, moved = jnp.where(keep, y, 0.0), jnp.where(keep, moved, 0.0)
        up_in[f, r, :, 0:c1] = y.astype(BF16)
        up_in[f, r, :, c1 : 2 * c1] = moved.astype(BF16)

    @pl.loop(0, frames)
    def _(f):
        for r in range(height):
            up_row(f, r, lat[f, r].astype(F32), None)
        up_row(f, height, lat_row[f].astype(F32), below_ok)

    fetches[1].wait()

    def tap(dy, dx, ky, kx):
        a = up_in[:, dy : dy + height, :, dx * c1 : (dx + 1) * c1].reshape(-1, c1)
        return jnp.dot(a, up_w[ky, kx], preferred_element_type=F32)

    lifted = {
        (0, 0): lambda: tap(0, 0, 1, 1),
        (0, 1): lambda: tap(0, 0, 1, 2) + tap(0, 1, 1, 0),
        (1, 0): lambda: tap(0, 0, 2, 1) + tap(1, 0, 0, 1),
        (1, 1): lambda: tap(0, 0, 2, 2) + tap(0, 1, 2, 0) + tap(1, 0, 0, 2) + tap(1, 1, 0, 0),
    }
    for (a, b), make in lifted.items():
        block = make().astype(BF16).reshape(frames, height, across, c2)
        for i in range(height):
            raw2[2 : 2 + frames, 1 + 2 * i + a, b * across : (b + 1) * across, :] = block[:, i]

    def norm_conv(i, raw, col, stage, st, gain, shift, w, w_copy):
        own = raw[2 : 2 + frames, 1 : 1 + out_h].astype(F32)
        set_stats(st, own.reshape(-1, c2))
        send_stats(st, i)
        copies = field_copies(i, raw, col, stage, 1) + field_copies(i, raw, col, stage, 0)
        start([c for c in copies if c[0] == (1, 0, 0)])
        for f in range(frames):
            for r in range(out_h):
                stage[0, f, r] = raw[2 + f, 1 + r, 0:16, :].astype(F32)[0:1]
                stage[1, f, r] = raw[2 + f, 1 + r, out_w - 16 : out_w, :].astype(F32)[15:16]
        start([c for c in copies if c[0][2] != 0 and c[0][1] == 0])
        start([c for c in copies if c[0][1] != 0])
        mean, factor, offset = affine(st, i, frames * out_h * out_w, gain, shift)

        def act(x):
            return half_silu((x - mean) * factor + offset)

        def one_row(f, r, keep):
            y = act(raw[f, r].astype(F32))
            left = jnp.where(left_ok, act(col[0, f, r]), 0.0)
            right = jnp.where(right_ok, act(col[1, f, r]), 0.0)
            even, odd = y[:across], y[across:]
            planes = (
                jnp.where(row_in == 0, left, pltpu.roll(odd, 1, 0)),
                even,
                odd,
                jnp.where(row_in == across - 1, right, pltpu.roll(even, across - 1, 0)),
            )
            for k, plane in enumerate(planes):
                if keep is not None:
                    plane = jnp.where(keep, plane, 0.0)
                conv_in[f, r, :, k * c2 : (k + 1) * c2] = plane.astype(BF16)

        def fill(rows, is_row):
            here = [c for c in copies if is_row(c[0][1])]
            received([c for c in here if c[0][0] == 0])

            @pl.loop(2, 2 + frames)
            def _(f):
                for r, keep in rows:
                    one_row(f, r, keep)

            @pl.when(ta == 0)
            def _():
                for f in range(2):
                    for r, _ in rows:
                        conv_in[f, r] = conv_in[2, r]

            received([c for c in here if c[0][0] == 1])

            @pl.when(ta > 0)
            def _():
                @pl.loop(0, 2)
                def _(f):
                    for r, keep in rows:
                        one_row(f, r, keep)

        def taps(b, rows):
            steps = [(dt, dy) for dy in rows for dt in range(3)]
            windows = [
                conv_in[dt : dt + frames, dy : dy + out_h, :, b * c2 : (b + 3) * c2]
                for dt, dy in steps
            ]
            window = jnp.concatenate([x.reshape(-1, 3 * c2) for x in windows], axis=1)
            weight = jnp.concatenate([w[dt, dy].reshape(3 * c2, c2) for dt, dy in steps], axis=0)
            return jnp.dot(window, weight, preferred_element_type=F32)

        fill([(r, None) for r in range(1, out_h + 1)], lambda dha: dha == 0)
        w_copy.wait()
        for b in range(2):
            acc[b] = taps(b, (1,))
        fill([(0, above_ok), (out_h + 1, below_ok)], lambda dha: dha != 0)
        totals = [acc[b] + taps(b, (0, 2)) for b in range(2)]
        return [total.reshape(frames, out_h, across, c2) for total in totals], copies

    hidden, copies2 = norm_conv(1, raw2, col2, stage2, st2, g2, s2, ca_w, fetches[8])
    for b in range(2):
        raw3[2 : 2 + frames, 1 : 1 + out_h, b * across : (b + 1) * across, :] = hidden[b].astype(
            BF16
        )
    branch, copies3 = norm_conv(2, raw3, col3, stage3, st3, g3, s3, cb_w, fetches[9])
    for b in range(2):
        lift = raw2[2 : 2 + frames, 1 : 1 + out_h, b * across : (b + 1) * across, :]
        total = lift.astype(F32) + branch[b]
        for k in range(c2 // 128):
            merged[k, :, :, pl.ds(b, across, stride=2), :] = total[..., k * 128 : (k + 1) * 128]
    for k in range(c2 // 128):
        out[:, :, :, k * 128 : (k + 1) * 128] = merged[k].astype(BF16)

    sent(lat_copies)
    sent(copies2)
    sent(copies3)
    for i, st in enumerate((st1, st2, st3)):
        all_stats(st, i, stat_send)


def per_device(sizes, lat, g1, s1, up_w, g2, s2, ca, g3, s3, cb):
    frames, height, across, c1 = lat.shape
    c2 = up_w.shape[-1]
    out_h, out_w = 2 * height, 2 * across
    n_all = sizes[0] * sizes[1] * sizes[2]
    vmem = pl.BlockSpec(memory_space=pltpu.VMEM)
    hbm = pl.BlockSpec(memory_space=pltpu.HBM)
    field = pltpu.VMEM((frames + 2, out_h + 2, out_w, c2), BF16)
    column = pltpu.VMEM((2, frames + 2, out_h + 2, 1, c2), F32)
    staged = pltpu.VMEM((2, frames, out_h, 1, c2), F32)
    macs = frames * out_h * out_w * 54 * c2 * c2 + frames * height * across * 9 * c1 * c2
    operands = [lat, g1[None], s1[None], up_w, g2[None], s2[None], ca, g3[None], s3[None], cb]
    operands = [pltpu.with_memory_space_constraint(x, pltpu.HBM) for x in operands]
    return pl.pallas_call(
        functools.partial(kernel, sizes),
        out_shape=jax.ShapeDtypeStruct((frames, out_h, out_w, c2), BF16),
        in_specs=[hbm] * 10,
        out_specs=vmem,
        scratch_shapes=[
            pltpu.VMEM(lat.shape, BF16),
            pltpu.VMEM((1, c1), F32),
            pltpu.VMEM((1, c1), F32),
            pltpu.VMEM(up_w.shape, BF16),
            pltpu.VMEM((1, c2), F32),
            pltpu.VMEM((1, c2), F32),
            pltpu.VMEM(ca.shape, BF16),
            pltpu.VMEM((1, c2), F32),
            pltpu.VMEM((1, c2), F32),
            pltpu.VMEM(cb.shape, BF16),
            pltpu.VMEM((frames, across, c1), BF16),
            pltpu.VMEM((frames, height + 1, 1, c1), F32),
            pltpu.VMEM((frames, height, 1, c1), F32),
            pltpu.VMEM((frames, height + 1, across, 2 * c1), BF16),
            field,
            field,
            column,
            column,
            staged,
            staged,
            pltpu.VMEM((frames + 2, out_h + 2, across, 4 * c2), BF16),
            pltpu.VMEM((2, frames * out_h * across, c2), F32),
            pltpu.VMEM((c2 // 128, frames, out_h, out_w, 128), F32),
            pltpu.VMEM((n_all, 2, c1), F32),
            pltpu.VMEM((n_all, 2, c2), F32),
            pltpu.VMEM((n_all, 2, c2), F32),
            pltpu.SemaphoreType.DMA((10,)),
            pltpu.SemaphoreType.DMA((3, 18)),
            pltpu.SemaphoreType.DMA((3, 18)),
            pltpu.SemaphoreType.DMA((3,)),
            pltpu.SemaphoreType.DMA((3,)),
        ],
        compiler_params=pltpu.CompilerParams(
            collective_id=0, has_side_effects=True, vmem_limit_bytes=44 * 2**20
        ),
        cost_estimate=pl.CostEstimate(
            flops=2 * macs, bytes_accessed=10_000_000, transcendentals=2_000_000
        ),
    )(*operands)


def solution(mesh):
    sizes = (mesh.shape["ha"], mesh.shape["wa"], mesh.shape["ta"])
    fields = P(("videos", "ta"), "ha", "wa", None)
    return jax.shard_map(
        functools.partial(per_device, sizes),
        mesh=mesh,
        in_specs=(fields,) + (P(),) * 9,
        out_specs=fields,
        check_vma=False,
    )
```

```python
import functools
import jax
import jax.numpy as jnp
from jax import lax
from jax.experimental import pallas as pl
from jax.experimental.pallas import tpu as pltpu
from jax.sharding import PartitionSpec as P

GROUPS = 32
EPSILON = 1e-06
MESH = pl.DeviceIdType.MESH
F32 = jnp.float32
BF16 = jnp.bfloat16


def group_moments(mean, squares, count, width):
    means, totals = [], []
    for k in range(mean.shape[1] // 128):
        m, q = (v[:, k * 128 : (k + 1) * 128] for v in (mean, squares))
        lane = lax.broadcasted_iota(jnp.int32, m.shape, 1)
        step = 1
        while step < width:
            low = (lane & step) == 0
            m_other, q_other = (
                jnp.where(low, pltpu.roll(v, 128 - step, 1), pltpu.roll(v, step, 1)) for v in (m, q)
            )
            gap = m - m_other
            q = q + q_other + gap * gap * (0.5 * count * step)
            m = 0.5 * (m + m_other)
            step *= 2
        means.append(m)
        totals.append(q)
    return jnp.concatenate(means, axis=1), jnp.concatenate(totals, axis=1)


def half_silu(h):
    return h + h * jnp.tanh(h)


def kernel(
    sizes,
    lat_hbm,
    g1_hbm,
    s1_hbm,
    up_hbm,
    g2_hbm,
    s2_hbm,
    ca_hbm,
    g3_hbm,
    s3_hbm,
    cb_hbm,
    out,
    lat,
    g1,
    s1,
    up_w,
    g2,
    s2,
    ca_w,
    g3,
    s3,
    cb_w,
    lat_row,
    lat_col,
    lat_stage,
    up_in,
    raw2,
    raw3,
    col2,
    col3,
    stage2,
    stage3,
    conv_in,
    acc,
    merged,
    st1,
    st2,
    st3,
    w_sem,
    halo_send,
    halo_recv,
    stat_send,
    stat_recv,
):
    n_ha, n_wa, n_ta = sizes
    n_all = n_ha * n_wa * n_ta
    ha, wa, ta = lax.axis_index("ha"), lax.axis_index("wa"), lax.axis_index("ta")
    frames, height, across, c1 = lat.shape
    c2 = up_w.shape[-1]
    out_h, out_w = 2 * height, 2 * across

    sources = (lat_hbm, up_hbm, g1_hbm, s1_hbm, g2_hbm, s2_hbm, g3_hbm, s3_hbm, ca_hbm, cb_hbm)
    places = (lat, up_w, g1, s1, g2, s2, g3, s3, ca_w, cb_w)
    fetches = [
        pltpu.make_async_copy(a, b, w_sem.at[i]) for i, (a, b) in enumerate(zip(sources, places))
    ]
    fetches[0].start()
    for fetch in fetches[2:8]:
        fetch.start()

    at_ha = [ha if d == 0 else lax.rem(ha + d, n_ha) for d in range(n_ha)]
    at_wa = [wa if d == 0 else lax.rem(wa + d, n_wa) for d in range(n_wa)]
    at_ta = [ta if d == 0 else lax.rem(ta + d, n_ta) for d in range(n_ta)]

    def peers():
        for slot in range(n_all - 1, 0, -1):
            h, w, t = slot // (n_wa * n_ta), slot // n_ta % n_wa, slot % n_ta
            yield slot, {"ha": at_ha[h], "wa": at_wa[w], "ta": at_ta[t]}

    barrier = pltpu.get_barrier_semaphore()
    for _, device in peers():
        pl.semaphore_signal(barrier, inc=1, device_id=device, device_id_type=MESH)

    def set_stats(st, x):
        rows = x.shape[0]
        mean = jnp.sum(x, axis=0, keepdims=True) * (1.0 / rows)
        centred = x - mean
        st[0, 0:1, :] = mean
        st[0, 1:2, :] = jnp.sum(centred * centred, axis=0, keepdims=True)

    def send_stats(st, i):
        for slot, device in peers():
            pltpu.make_async_remote_copy(
                src_ref=st.at[0],
                dst_ref=st.at[slot],
                send_sem=stat_send.at[i],
                recv_sem=stat_recv.at[i],
                device_id=device,
                device_id_type=MESH,
            ).start()

    def all_stats(st, i, sem):
        pltpu.make_async_copy(st.at[1:n_all], st.at[1:n_all], sem.at[i]).wait()

    def affine(st, i, rows, gain, shift):
        all_stats(st, i, stat_recv)
        c = st.shape[-1]
        width = c // GROUPS
        v = st[...]
        mean_c = jnp.sum(v, axis=0) * (1.0 / n_all)
        kind = lax.broadcasted_iota(jnp.int32, v.shape, 1)
        off = v - mean_c[0:1][None]
        parts = jnp.sum(jnp.where(kind == 0, off * off * float(rows), v), axis=0)
        mean, squares = group_moments(
            jnp.broadcast_to(mean_c[0:1], (8, c)),
            jnp.broadcast_to(parts[0:1] + parts[1:2], (8, c)),
            float(rows * n_all),
            width,
        )
        spread = squares * (1.0 / (width * rows * n_all))
        scaling = lax.rsqrt(spread + EPSILON)
        factor = 0.5 * scaling[0:1] * gain[...]
        return mean[0:1], factor, 0.5 * shift[...]

    def inside(dta, dha, dwa):
        h, w, t = ha + dha, wa + dwa, ta + dta
        ok = (h >= 0) & (h < n_ha) & (w >= 0) & (w < n_wa)
        return ok & (t >= 0) & (t < n_ta)

    def neighbour(dta, dha, dwa):
        return {"ha": ha + dha, "wa": wa + dwa, "ta": ta + dta}

    def remote(src, dst, i, move):
        dta, dha, dwa = move
        k = dta * 9 + (dha + 1) * 3 + dwa + 1
        return pltpu.make_async_remote_copy(
            src_ref=src,
            dst_ref=dst,
            send_sem=halo_send.at[i, k],
            recv_sem=halo_recv.at[i, k],
            device_id=neighbour(*move),
            device_id_type=MESH,
        )

    def start(copies):
        for move, copy in copies:
            pl.when(inside(*move))(copy.start)

    def sent(copies):
        for move, copy in copies:
            pl.when(inside(*move))(copy.wait_send)

    def received(copies):
        for move, copy in copies:
            dta, dha, dwa = move
            pl.when(inside(-dta, -dha, -dwa))(copy.wait_recv)

    def field_copies(i, raw, col, stage, dta):
        copies = []
        f_from, f_to, count = (0, 2, frames) if dta == 0 else (frames - 2, 0, 2)
        for dha in (-1, 0, 1):
            r_from, r_to, n_r = {-1: (0, out_h + 1, 1), 0: (0, 1, out_h), 1: (out_h - 1, 0, 1)}[dha]
            for dwa in (0, -1, 1):
                move = (dta, dha, dwa)
                if move == (0, 0, 0):
                    continue
                fd, rd = pl.ds(f_to, count), pl.ds(r_to, n_r)
                if dwa == 0:
                    src = raw.at[pl.ds(f_from + 2, count), pl.ds(r_from + 1, n_r)]
                    dst = raw.at[fd, rd]
                else:
                    side = (dwa + 1) // 2
                    src = stage.at[side, pl.ds(f_from, count), pl.ds(r_from, n_r)]
                    dst = col.at[1 - side, fd, rd]
                copies.append((move, remote(src, dst, i, move)))
        return copies

    fetches[0].wait()
    for i in (1, 8, 9):
        fetches[i].start()
    set_stats(st1, lat[...].astype(F32).reshape(-1, c1))
    for f in range(frames):
        for r in range(height):
            lat_stage[f, r] = lat[f, r, 0:16, :].astype(F32)[0:1]
    pl.semaphore_wait(barrier, n_all - 1)
    send_stats(st1, 0)
    lat_copies = [
        ((0, -1, 0), remote(lat.at[:, 0], lat_row, 0, (0, -1, 0))),
        ((0, 0, -1), remote(lat_stage, lat_col.at[:, pl.ds(0, height)], 0, (0, 0, -1))),
        (
            (0, -1, -1),
            remote(
                lat_stage.at[:, pl.ds(0, 1)], lat_col.at[:, pl.ds(height, 1)], 0, (0, -1, -1)
            ),
        ),
    ]
    start(lat_copies)
    for fetch in fetches[2:8]:
        fetch.wait()
    mean, factor, offset = affine(st1, 0, frames * height * across, g1, s1)
    received(lat_copies)
    row_in = lax.broadcasted_iota(jnp.int32, (across, 1), 0)
    right_ok, left_ok = wa < n_wa - 1, wa > 0
    below_ok, above_ok = ha < n_ha - 1, ha > 0

    def up_row(f, r, x, keep):
        y = half_silu((x - mean) * factor + offset)
        edge = half_silu((lat_col[f, r] - mean) * factor + offset)
        edge = jnp.where(right_ok, edge, 0.0)
        moved = jnp.where(row_in == across - 1, edge, pltpu.roll(y, across - 1, 0))
        if keep is not None:
            y, moved = jnp.where(keep, y, 0.0), jnp.where(keep, moved, 0.0)
        up_in[f, r, :, 0:c1] = y.astype(BF16)
        up_in[f, r, :, c1 : 2 * c1] = moved.astype(BF16)

    @pl.loop(0, frames)
    def _(f):
        for r in range(height):
            up_row(f, r, lat[f, r].astype(F32), None)
        up_row(f, height, lat_row[f].astype(F32), below_ok)

    fetches[1].wait()

    def tap(dy, dx, ky, kx):
        a = up_in[:, dy : dy + height, :, dx * c1 : (dx + 1) * c1].reshape(-1, c1)
        return jnp.dot(a, up_w[ky, kx], preferred_element_type=F32)

    lifted = {
        (0, 0): lambda: tap(0, 0, 1, 1),
        (0, 1): lambda: tap(0, 0, 1, 2) + tap(0, 1, 1, 0),
        (1, 0): lambda: tap(0, 0, 2, 1) + tap(1, 0, 0, 1),
        (1, 1): lambda: tap(0, 0, 2, 2) + tap(0, 1, 2, 0) + tap(1, 0, 0, 2) + tap(1, 1, 0, 0),
    }
    for (a, b), make in lifted.items():
        block = make().astype(BF16).reshape(frames, height, across, c2)
        for i in range(height):
            raw2[2 : 2 + frames, 1 + 2 * i + a, b * across : (b + 1) * across, :] = block[:, i]

    def norm_conv(i, raw, col, stage, st, gain, shift, w, w_copy, finish):
        own = raw[2 : 2 + frames, 1 : 1 + out_h].astype(F32)
        set_stats(st, own.reshape(-1, c2))
        send_stats(st, i)
        copies = field_copies(i, raw, col, stage, 1) + field_copies(i, raw, col, stage, 0)
        start([c for c in copies if c[0] == (1, 0, 0)])
        for f in range(frames):
            for r in range(out_h):
                stage[0, f, r] = raw[2 + f, 1 + r, 0:16, :].astype(F32)[0:1]
                stage[1, f, r] = raw[2 + f, 1 + r, out_w - 16 : out_w, :].astype(F32)[15:16]
        start([c for c in copies if c[0][2] != 0 and c[0][1] == 0])
        start([c for c in copies if c[0][1] != 0])
        mean, factor, offset = affine(st, i, frames * out_h * out_w, gain, shift)

        def act(x):
            return half_silu((x - mean) * factor + offset)

        def one_row(f, r, keep):
            y = act(raw[f, r].astype(F32))
            left = jnp.where(left_ok, act(col[0, f, r]), 0.0)
            right = jnp.where(right_ok, act(col[1, f, r]), 0.0)
            even, odd = y[:across], y[across:]
            planes = (
                jnp.where(row_in == 0, left, pltpu.roll(odd, 1, 0)),
                even,
                odd,
                jnp.where(row_in == across - 1, right, pltpu.roll(even, across - 1, 0)),
            )
            for k, plane in enumerate(planes):
                if keep is not None:
                    plane = jnp.where(keep, plane, 0.0)
                conv_in[f, r, :, k * c2 : (k + 1) * c2] = plane.astype(BF16)

        def fill(rows, is_row):
            here = [c for c in copies if is_row(c[0][1])]
            received([c for c in here if c[0][0] == 0])

            @pl.loop(2, 2 + frames)
            def _(f):
                for r, keep in rows:
                    one_row(f, r, keep)

            @pl.when(ta == 0)
            def _():
                for f in range(2):
                    for r, _ in rows:
                        conv_in[f, r] = conv_in[2, r]

            received([c for c in here if c[0][0] == 1])

            @pl.when(ta > 0)
            def _():
                @pl.loop(0, 2)
                def _(f):
                    for r, keep in rows:
                        one_row(f, r, keep)

        def taps(f, rows, total):
            for dy in rows:
                for dt in range(3):
                    here = conv_in.at[f + dt, dy : dy + out_h]
                    sides = [here[:, :, b * c2 : (b + 3) * c2] for b in range(2)]
                    part = jnp.dot(
                        jnp.concatenate([x.reshape(-1, 3 * c2) for x in sides], axis=0),
                        w[dt, dy].reshape(3 * c2, c2),
                        preferred_element_type=F32,
                    )
                    total = part if total is None else total + part
            return total

        fill([(r, None) for r in range(1, out_h + 1)], lambda dha: dha == 0)
        w_copy.wait()
        for f in range(frames):
            acc[f] = taps(f, (1,), None)
        fill([(0, above_ok), (out_h + 1, below_ok)], lambda dha: dha != 0)
        for f in range(frames):
            finish(f, taps(f, (0, 2), acc[f]).reshape(2, out_h, across, c2))
        return copies

    def keep_hidden(f, hidden):
        for b in range(2):
            raw3[2 + f, 1 : 1 + out_h, b * across : (b + 1) * across, :] = hidden[b].astype(BF16)

    def merge(f, branch):
        for b in range(2):
            lift = raw2[2 + f, 1 : 1 + out_h, b * across : (b + 1) * across, :]
            total = lift.astype(F32) + branch[b]
            for k in range(c2 // 128):
                lanes = slice(k * 128, (k + 1) * 128)
                merged[k, f, :, pl.ds(b, across, stride=2), :] = total[..., lanes]
        for k in range(c2 // 128):
            out[f, :, :, k * 128 : (k + 1) * 128] = merged[k, f].astype(BF16)

    copies2 = norm_conv(1, raw2, col2, stage2, st2, g2, s2, ca_w, fetches[8], keep_hidden)
    copies3 = norm_conv(2, raw3, col3, stage3, st3, g3, s3, cb_w, fetches[9], merge)

    sent(lat_copies)
    sent(copies2)
    sent(copies3)
    for i, st in enumerate((st1, st2, st3)):
        all_stats(st, i, stat_send)


def per_device(sizes, lat, g1, s1, up_w, g2, s2, ca, g3, s3, cb):
    frames, height, across, c1 = lat.shape
    c2 = up_w.shape[-1]
    out_h, out_w = 2 * height, 2 * across
    n_all = sizes[0] * sizes[1] * sizes[2]
    vmem = pl.BlockSpec(memory_space=pltpu.VMEM)
    hbm = pl.BlockSpec(memory_space=pltpu.HBM)
    field = pltpu.VMEM((frames + 2, out_h + 2, out_w, c2), BF16)
    column = pltpu.VMEM((2, frames + 2, out_h + 2, 1, c2), F32)
    staged = pltpu.VMEM((2, frames, out_h, 1, c2), F32)
    macs = frames * out_h * out_w * 54 * c2 * c2 + frames * height * across * 9 * c1 * c2
    operands = [lat, g1[None], s1[None], up_w, g2[None], s2[None], ca, g3[None], s3[None], cb]
    operands = [pltpu.with_memory_space_constraint(x, pltpu.HBM) for x in operands]
    return pl.pallas_call(
        functools.partial(kernel, sizes),
        out_shape=jax.ShapeDtypeStruct((frames, out_h, out_w, c2), BF16),
        in_specs=[hbm] * 10,
        out_specs=vmem,
        scratch_shapes=[
            pltpu.VMEM(lat.shape, BF16),
            pltpu.VMEM((1, c1), F32),
            pltpu.VMEM((1, c1), F32),
            pltpu.VMEM(up_w.shape, BF16),
            pltpu.VMEM((1, c2), F32),
            pltpu.VMEM((1, c2), F32),
            pltpu.VMEM(ca.shape, BF16),
            pltpu.VMEM((1, c2), F32),
            pltpu.VMEM((1, c2), F32),
            pltpu.VMEM(cb.shape, BF16),
            pltpu.VMEM((frames, across, c1), BF16),
            pltpu.VMEM((frames, height + 1, 1, c1), F32),
            pltpu.VMEM((frames, height, 1, c1), F32),
            pltpu.VMEM((frames, height + 1, across, 2 * c1), BF16),
            field,
            field,
            column,
            column,
            staged,
            staged,
            pltpu.VMEM((frames + 2, out_h + 2, across, 4 * c2), BF16),
            pltpu.VMEM((frames, out_h * out_w, c2), F32),
            pltpu.VMEM((c2 // 128, frames, out_h, out_w, 128), F32),
            pltpu.VMEM((n_all, 2, c1), F32),
            pltpu.VMEM((n_all, 2, c2), F32),
            pltpu.VMEM((n_all, 2, c2), F32),
            pltpu.SemaphoreType.DMA((10,)),
            pltpu.SemaphoreType.DMA((3, 18)),
            pltpu.SemaphoreType.DMA((3, 18)),
            pltpu.SemaphoreType.DMA((3,)),
            pltpu.SemaphoreType.DMA((3,)),
        ],
        compiler_params=pltpu.CompilerParams(
            collective_id=0, has_side_effects=True, vmem_limit_bytes=44 * 2**20
        ),
        cost_estimate=pl.CostEstimate(
            flops=2 * macs, bytes_accessed=10_000_000, transcendentals=2_000_000
        ),
    )(*operands)


def solution(mesh):
    sizes = (mesh.shape["ha"], mesh.shape["wa"], mesh.shape["ta"])
    fields = P(("videos", "ta"), "ha", "wa", None)
    return jax.shard_map(
        functools.partial(per_device, sizes),
        mesh=mesh,
        in_specs=(fields,) + (P(),) * 9,
        out_specs=fields,
        check_vma=False,
    )
```

```python
import functools
import jax
import jax.numpy as jnp
from jax import lax
from jax.experimental import pallas as pl
from jax.experimental.pallas import tpu as pltpu
from jax.sharding import PartitionSpec as P

GROUPS = 32
EPSILON = 1e-06
MESH = pl.DeviceIdType.MESH
F32 = jnp.float32
BF16 = jnp.bfloat16


def group_moments(mean, squares, count, width):
    means, totals = [], []
    for k in range(mean.shape[1] // 128):
        m, q = (v[:, k * 128 : (k + 1) * 128] for v in (mean, squares))
        lane = lax.broadcasted_iota(jnp.int32, m.shape, 1)
        step = 1
        while step < width:
            low = (lane & step) == 0
            m_other, q_other = (
                jnp.where(low, pltpu.roll(v, 128 - step, 1), pltpu.roll(v, step, 1)) for v in (m, q)
            )
            gap = m - m_other
            q = q + q_other + gap * gap * (0.5 * count * step)
            m = 0.5 * (m + m_other)
            step *= 2
        means.append(m)
        totals.append(q)
    return jnp.concatenate(means, axis=1), jnp.concatenate(totals, axis=1)


def half_silu(h):
    return h + h * jnp.tanh(h)


def kernel(
    sizes,
    lat_hbm,
    g1_hbm,
    s1_hbm,
    up_hbm,
    g2_hbm,
    s2_hbm,
    ca_hbm,
    g3_hbm,
    s3_hbm,
    cb_hbm,
    out,
    lat,
    g1,
    s1,
    up_w,
    g2,
    s2,
    ca_w,
    g3,
    s3,
    cb_w,
    lat_row,
    lat_col,
    lat_stage,
    up_in,
    raw2,
    raw3,
    col2,
    col3,
    stage2,
    stage3,
    conv_in,
    acc,
    merged,
    st1,
    st2,
    st3,
    w_sem,
    halo_send,
    halo_recv,
    stat_send,
    stat_recv,
):
    n_ha, n_wa, n_ta = sizes
    n_all = n_ha * n_wa * n_ta
    ha, wa, ta = lax.axis_index("ha"), lax.axis_index("wa"), lax.axis_index("ta")
    frames, height, across, c1 = lat.shape
    c2 = up_w.shape[-1]
    out_h, out_w = 2 * height, 2 * across

    sources = (lat_hbm, up_hbm, g1_hbm, s1_hbm, g2_hbm, s2_hbm, g3_hbm, s3_hbm, ca_hbm, cb_hbm)
    places = (lat, up_w, g1, s1, g2, s2, g3, s3, ca_w, cb_w)
    fetches = [
        pltpu.make_async_copy(a, b, w_sem.at[i]) for i, (a, b) in enumerate(zip(sources, places))
    ]
    fetches[0].start()
    for fetch in fetches[2:8]:
        fetch.start()

    at_ha = [ha if d == 0 else lax.rem(ha + d, n_ha) for d in range(n_ha)]
    at_wa = [wa if d == 0 else lax.rem(wa + d, n_wa) for d in range(n_wa)]
    at_ta = [ta if d == 0 else lax.rem(ta + d, n_ta) for d in range(n_ta)]

    def peers():
        for slot in range(n_all - 1, 0, -1):
            h, w, t = slot // (n_wa * n_ta), slot // n_ta % n_wa, slot % n_ta
            yield slot, {"ha": at_ha[h], "wa": at_wa[w], "ta": at_ta[t]}

    barrier = pltpu.get_barrier_semaphore()
    for _, device in peers():
        pl.semaphore_signal(barrier, inc=1, device_id=device, device_id_type=MESH)

    def set_stats(st, x):
        rows = x.shape[0]
        mean = jnp.sum(x, axis=0, keepdims=True) * (1.0 / rows)
        centred = x - mean
        st[0, 0:1, :] = mean
        st[0, 1:2, :] = jnp.sum(centred * centred, axis=0, keepdims=True)

    def send_stats(st, i):
        for slot, device in peers():
            pltpu.make_async_remote_copy(
                src_ref=st.at[0],
                dst_ref=st.at[slot],
                send_sem=stat_send.at[i],
                recv_sem=stat_recv.at[i],
                device_id=device,
                device_id_type=MESH,
            ).start()

    def all_stats(st, i, sem):
        pltpu.make_async_copy(st.at[1:n_all], st.at[1:n_all], sem.at[i]).wait()

    def affine(st, i, rows, gain, shift):
        all_stats(st, i, stat_recv)
        c = st.shape[-1]
        width = c // GROUPS
        v = st[...]
        mean_c = jnp.sum(v, axis=0) * (1.0 / n_all)
        kind = lax.broadcasted_iota(jnp.int32, v.shape, 1)
        off = v - mean_c[0:1][None]
        parts = jnp.sum(jnp.where(kind == 0, off * off * float(rows), v), axis=0)
        mean, squares = group_moments(
            jnp.broadcast_to(mean_c[0:1], (8, c)),
            jnp.broadcast_to(parts[0:1] + parts[1:2], (8, c)),
            float(rows * n_all),
            width,
        )
        spread = squares * (1.0 / (width * rows * n_all))
        scaling = lax.rsqrt(spread + EPSILON)
        factor = 0.5 * scaling[0:1] * gain[...]
        return mean[0:1], factor, 0.5 * shift[...]

    def inside(dta, dha, dwa):
        h, w, t = ha + dha, wa + dwa, ta + dta
        ok = (h >= 0) & (h < n_ha) & (w >= 0) & (w < n_wa)
        return ok & (t >= 0) & (t < n_ta)

    def neighbour(dta, dha, dwa):
        return {"ha": ha + dha, "wa": wa + dwa, "ta": ta + dta}

    def remote(src, dst, i, move):
        dta, dha, dwa = move
        k = dta * 9 + (dha + 1) * 3 + dwa + 1
        return pltpu.make_async_remote_copy(
            src_ref=src,
            dst_ref=dst,
            send_sem=halo_send.at[i, k],
            recv_sem=halo_recv.at[i, k],
            device_id=neighbour(*move),
            device_id_type=MESH,
        )

    def start(copies):
        for move, copy in copies:
            pl.when(inside(*move))(copy.start)

    def sent(copies):
        for move, copy in copies:
            pl.when(inside(*move))(copy.wait_send)

    def received(copies):
        for move, copy in copies:
            dta, dha, dwa = move
            pl.when(inside(-dta, -dha, -dwa))(copy.wait_recv)

    def field_copies(i, raw, col, stage, dta):
        copies = []
        f_from, f_to, count = (0, 2, frames) if dta == 0 else (frames - 2, 0, 2)
        for dha in (-1, 0, 1):
            r_from, r_to, n_r = {-1: (0, out_h + 1, 1), 0: (0, 1, out_h), 1: (out_h - 1, 0, 1)}[dha]
            for dwa in (0, -1, 1):
                move = (dta, dha, dwa)
                if move == (0, 0, 0):
                    continue
                fd, rd = pl.ds(f_to, count), pl.ds(r_to, n_r)
                if dwa == 0:
                    src = raw.at[pl.ds(f_from + 2, count), pl.ds(r_from + 1, n_r)]
                    dst = raw.at[fd, rd]
                else:
                    side = (dwa + 1) // 2
                    src = stage.at[side, pl.ds(f_from, count), pl.ds(r_from, n_r)]
                    dst = col.at[1 - side, fd, rd]
                copies.append((move, remote(src, dst, i, move)))
        return copies

    fetches[0].wait()
    for i in (1, 8, 9):
        fetches[i].start()
    set_stats(st1, lat[...].astype(F32).reshape(-1, c1))
    for f in range(frames):
        for r in range(height):
            lat_stage[f, r] = lat[f, r, 0:16, :].astype(F32)[0:1]
    pl.semaphore_wait(barrier, n_all - 1)
    send_stats(st1, 0)
    lat_copies = [
        ((0, -1, 0), remote(lat.at[:, 0], lat_row, 0, (0, -1, 0))),
        ((0, 0, -1), remote(lat_stage, lat_col.at[:, pl.ds(0, height)], 0, (0, 0, -1))),
        (
            (0, -1, -1),
            remote(
                lat_stage.at[:, pl.ds(0, 1)], lat_col.at[:, pl.ds(height, 1)], 0, (0, -1, -1)
            ),
        ),
    ]
    start(lat_copies)
    for fetch in fetches[2:8]:
        fetch.wait()
    mean, factor, offset = affine(st1, 0, frames * height * across, g1, s1)
    received(lat_copies)
    row_in = lax.broadcasted_iota(jnp.int32, (across, 1), 0)
    right_ok, left_ok = wa < n_wa - 1, wa > 0
    below_ok, above_ok = ha < n_ha - 1, ha > 0

    def up_row(f, r, x, keep):
        y = half_silu((x - mean) * factor + offset)
        edge = half_silu((lat_col[f, r] - mean) * factor + offset)
        edge = jnp.where(right_ok, edge, 0.0)
        moved = jnp.where(row_in == across - 1, edge, pltpu.roll(y, across - 1, 0))
        if keep is not None:
            y, moved = jnp.where(keep, y, 0.0), jnp.where(keep, moved, 0.0)
        up_in[f, r, :, 0:c1] = y.astype(BF16)
        up_in[f, r, :, c1 : 2 * c1] = moved.astype(BF16)

    @pl.loop(0, frames)
    def _(f):
        for r in range(height):
            up_row(f, r, lat[f, r].astype(F32), None)
        up_row(f, height, lat_row[f].astype(F32), below_ok)

    fetches[1].wait()

    def tap(dy, dx, ky, kx):
        a = up_in[:, dy : dy + height, :, dx * c1 : (dx + 1) * c1].reshape(-1, c1)
        return jnp.dot(a, up_w[ky, kx], preferred_element_type=F32)

    lifted = {
        (0, 0): lambda: tap(0, 0, 1, 1),
        (0, 1): lambda: tap(0, 0, 1, 2) + tap(0, 1, 1, 0),
        (1, 0): lambda: tap(0, 0, 2, 1) + tap(1, 0, 0, 1),
        (1, 1): lambda: tap(0, 0, 2, 2) + tap(0, 1, 2, 0) + tap(1, 0, 0, 2) + tap(1, 1, 0, 0),
    }
    for (a, b), make in lifted.items():
        block = make().astype(BF16).reshape(frames, height, across, c2)
        for i in range(height):
            raw2[2 : 2 + frames, 1 + 2 * i + a, b * across : (b + 1) * across, :] = block[:, i]

    def norm_conv(i, raw, col, stage, st, gain, shift, w, w_copy, finish):
        own = raw[2 : 2 + frames, 1 : 1 + out_h].astype(F32)
        set_stats(st, own.reshape(-1, c2))
        send_stats(st, i)
        copies = field_copies(i, raw, col, stage, 1) + field_copies(i, raw, col, stage, 0)
        start([c for c in copies if c[0] == (1, 0, 0)])
        for f in range(frames):
            for r in range(out_h):
                stage[0, f, r] = raw[2 + f, 1 + r, 0:16, :].astype(F32)[0:1]
                stage[1, f, r] = raw[2 + f, 1 + r, out_w - 16 : out_w, :].astype(F32)[15:16]
        start([c for c in copies if c[0][2] != 0 and c[0][1] == 0])
        start([c for c in copies if c[0][1] != 0])
        mean, factor, offset = affine(st, i, frames * out_h * out_w, gain, shift)

        def act(x):
            return half_silu((x - mean) * factor + offset)

        def one_row(f, r, keep):
            y = act(raw[f, r].astype(F32))
            left = jnp.where(left_ok, act(col[0, f, r]), 0.0)
            right = jnp.where(right_ok, act(col[1, f, r]), 0.0)
            even, odd = y[:across], y[across:]
            planes = (
                jnp.where(row_in == 0, left, pltpu.roll(odd, 1, 0)),
                even,
                odd,
                jnp.where(row_in == across - 1, right, pltpu.roll(even, across - 1, 0)),
            )
            for k, plane in enumerate(planes):
                if keep is not None:
                    plane = jnp.where(keep, plane, 0.0)
                conv_in[f, r, :, k * c2 : (k + 1) * c2] = plane.astype(BF16)

        def fill(rows, is_row):
            here = [c for c in copies if is_row(c[0][1])]
            received([c for c in here if c[0][0] == 0])

            @pl.loop(2, 2 + frames)
            def _(f):
                for r, keep in rows:
                    one_row(f, r, keep)

            @pl.when(ta == 0)
            def _():
                for f in range(2):
                    for r, _ in rows:
                        conv_in[f, r] = conv_in[2, r]

            received([c for c in here if c[0][0] == 1])

            @pl.when(ta > 0)
            def _():
                @pl.loop(0, 2)
                def _(f):
                    for r, keep in rows:
                        one_row(f, r, keep)

        def taps(b, dy, total):
            for dt in range(3):
                window = conv_in[dt : dt + frames, dy : dy + out_h, :, b * c2 : (b + 3) * c2]
                part = jnp.dot(
                    window.reshape(-1, 3 * c2),
                    w[dt, dy].reshape(3 * c2, c2),
                    preferred_element_type=F32,
                )
                total = part if total is None else total + part
            return total

        fill([(r, None) for r in range(1, out_h + 1)], lambda dha: dha == 0)
        w_copy.wait()
        for b in range(2):
            acc[b] = taps(b, 1, None)
        fill([(0, above_ok), (out_h + 1, below_ok)], lambda dha: dha != 0)
        for b in range(2):
            finish(b, taps(b, 2, taps(b, 0, acc[b])).reshape(frames, out_h, across, c2))
        return copies

    def keep_hidden(b, hidden):
        raw3[2 : 2 + frames, 1 : 1 + out_h, b * across : (b + 1) * across, :] = hidden.astype(BF16)

    def merge(b, branch):
        lift = raw2[2 : 2 + frames, 1 : 1 + out_h, b * across : (b + 1) * across, :]
        total = lift.astype(F32) + branch
        for k in range(c2 // 128):
            merged[k, :, :, pl.ds(b, across, stride=2), :] = total[..., k * 128 : (k + 1) * 128]

    copies2 = norm_conv(1, raw2, col2, stage2, st2, g2, s2, ca_w, fetches[8], keep_hidden)
    copies3 = norm_conv(2, raw3, col3, stage3, st3, g3, s3, cb_w, fetches[9], merge)
    for k in range(c2 // 128):
        out[:, :, :, k * 128 : (k + 1) * 128] = merged[k].astype(BF16)

    sent(lat_copies)
    sent(copies2)
    sent(copies3)
    for i, st in enumerate((st1, st2, st3)):
        all_stats(st, i, stat_send)


def per_device(sizes, lat, g1, s1, up_w, g2, s2, ca, g3, s3, cb):
    frames, height, across, c1 = lat.shape
    c2 = up_w.shape[-1]
    out_h, out_w = 2 * height, 2 * across
    n_all = sizes[0] * sizes[1] * sizes[2]
    vmem = pl.BlockSpec(memory_space=pltpu.VMEM)
    hbm = pl.BlockSpec(memory_space=pltpu.HBM)
    field = pltpu.VMEM((frames + 2, out_h + 2, out_w, c2), BF16)
    column = pltpu.VMEM((2, frames + 2, out_h + 2, 1, c2), F32)
    staged = pltpu.VMEM((2, frames, out_h, 1, c2), F32)
    macs = frames * out_h * out_w * 54 * c2 * c2 + frames * height * across * 9 * c1 * c2
    operands = [lat, g1[None], s1[None], up_w, g2[None], s2[None], ca, g3[None], s3[None], cb]
    operands = [pltpu.with_memory_space_constraint(x, pltpu.HBM) for x in operands]
    return pl.pallas_call(
        functools.partial(kernel, sizes),
        out_shape=jax.ShapeDtypeStruct((frames, out_h, out_w, c2), BF16),
        in_specs=[hbm] * 10,
        out_specs=vmem,
        scratch_shapes=[
            pltpu.VMEM(lat.shape, BF16),
            pltpu.VMEM((1, c1), F32),
            pltpu.VMEM((1, c1), F32),
            pltpu.VMEM(up_w.shape, BF16),
            pltpu.VMEM((1, c2), F32),
            pltpu.VMEM((1, c2), F32),
            pltpu.VMEM(ca.shape, BF16),
            pltpu.VMEM((1, c2), F32),
            pltpu.VMEM((1, c2), F32),
            pltpu.VMEM(cb.shape, BF16),
            pltpu.VMEM((frames, across, c1), BF16),
            pltpu.VMEM((frames, height + 1, 1, c1), F32),
            pltpu.VMEM((frames, height, 1, c1), F32),
            pltpu.VMEM((frames, height + 1, across, 2 * c1), BF16),
            field,
            field,
            column,
            column,
            staged,
            staged,
            pltpu.VMEM((frames + 2, out_h + 2, across, 4 * c2), BF16),
            pltpu.VMEM((2, frames * out_h * across, c2), F32),
            pltpu.VMEM((c2 // 128, frames, out_h, out_w, 128), F32),
            pltpu.VMEM((n_all, 2, c1), F32),
            pltpu.VMEM((n_all, 2, c2), F32),
            pltpu.VMEM((n_all, 2, c2), F32),
            pltpu.SemaphoreType.DMA((10,)),
            pltpu.SemaphoreType.DMA((3, 18)),
            pltpu.SemaphoreType.DMA((3, 18)),
            pltpu.SemaphoreType.DMA((3,)),
            pltpu.SemaphoreType.DMA((3,)),
        ],
        compiler_params=pltpu.CompilerParams(
            collective_id=0, has_side_effects=True, vmem_limit_bytes=44 * 2**20
        ),
        cost_estimate=pl.CostEstimate(
            flops=2 * macs, bytes_accessed=10_000_000, transcendentals=2_000_000
        ),
    )(*operands)


def solution(mesh):
    sizes = (mesh.shape["ha"], mesh.shape["wa"], mesh.shape["ta"])
    fields = P(("videos", "ta"), "ha", "wa", None)
    return jax.shard_map(
        functools.partial(per_device, sizes),
        mesh=mesh,
        in_specs=(fields,) + (P(),) * 9,
        out_specs=fields,
        check_vma=False,
    )
```
